32 devices in a mesh: seg: 4 (over z_hi, core), shard: 4 (over y, x), tok: 2 (over z_lo).
Axes of the slice: x: 2, y: 2, z: 4 (z_hi: 2, z_lo: 2; z = z_hi * 2 + z_lo), core: 2. Of those that a mesh axis runs over, the one named last changes fastest.
Arguments:
- activations: bfloat16 [768, 2560], P('tok', 'shard'), may hold values from -6 to 6
- gate_weight: bfloat16 [2560, 10240], P('shard', 'seg'), may hold values from -0.125 to 0.125
- up_weight: bfloat16 [2560, 10240], P('shard', 'seg'), may hold values from -0.125 to 0.125
- down_weight: bfloat16 [10240, 2560], P('seg', 'shard'), may hold values from -0.0625 to 0.0625
- encoder_weight: bfloat16 [2560, 8192], P(None, ('seg', 'shard')), may hold values from -0.125 to 0.125
- encoder_bias: float32 [8192], P(('seg', 'shard')), may hold values from -0.6 to 0.2
- decoder_weight: bfloat16 [8192, 2560], P(('seg', 'shard')), may hold values from -0.125 to 0.125
- decoder_bias: float32 [2560], replicated, may hold values from -1.5 to 1.5
- segment_sizes: int32 [4], replicated, may hold values from 1024 to 2048, as said below
Outputs:
- grad_encoder: float32 [2560, 8192], P('tok', ('seg', 'shard'))
- grad_decoder: float32 [8192, 2560], P(('seg', 'shard'), 'tok')
- prefix_mse: float32 [4], P('seg')
The draws below stay inside these ranges and needn't reach their ends.
Inputs may be any that keep to these rules, and one draw needn't show every extreme that they name: `segment_sizes`: at least one segment has all 2048 latents live.
All inputs are finite; a program needn't handle non-finite values.
Results may differ from the reference program's by a relative error of at most 0.0078.
Values may be sent and summed in bfloat16 or wider, within the bound.
A program may use at most 64 MiB of HBM per device.

```python
import math
import jax
import jax.numpy as jnp

D = 2560
FF = 10240
NSEG = 4
SEG_LAT = 2048
LATENTS = 8192
TOKENS = 768


def draw_segment_sizes(key, part):
    base = jax.random.fold_in(key, 11)
    size_key, pick_key = jax.random.split(base)
    sizes = jax.random.randint(size_key, (NSEG,), SEG_LAT // 2, SEG_LAT + 1)
    full_at = jax.random.randint(pick_key, (), 0, NSEG)
    return jnp.where(jnp.arange(NSEG) == full_at, SEG_LAT, sizes).astype(jnp.int32)


def shard_levels(stream_key, extent, cuts, least, top_value):
    gain = 1.0
    for axis_at, parts in cuts:
        draws = jax.random.uniform(jax.random.fold_in(jax.random.fold_in(stream_key, 6), axis_at), (parts,), jnp.float32, least / len(cuts), top_value / len(cuts))
        gain = gain * jnp.repeat(jnp.exp(draws), extent[axis_at] // parts).reshape((-1,) + (1,) * (len(extent) - 1 - axis_at))
    return gain


def noise(stream_key, dims, scale, reach, cuts=(), kind=jnp.bfloat16):
    level = shard_levels(stream_key, dims, cuts, -0.22, 0.18) if cuts else 1.0
    entries = jax.random.normal(stream_key, dims, jnp.float32) * scale * level
    return jnp.minimum(jnp.maximum(entries, -reach), reach).astype(kind)


def setup_inputs(seed: int = 0) -> dict:
    keys = jax.random.split(jax.random.key(seed), 10)
    activations = noise(keys[0], (TOKENS, D), 1.0, 6.0, ((0, 2), (1, 4)))
    gate_weight = noise(keys[1], (D, FF), D ** -0.5, 0.125, ((0, 4), (1, 4)))
    up_weight = noise(keys[2], (D, FF), D ** -0.5, 0.125, ((0, 4), (1, 4)))
    down_weight = noise(keys[3], (FF, D), FF ** -0.5, 0.0625, ((0, 4), (1, 4)))
    encoder_weight = noise(keys[4], (D, LATENTS), D ** -0.5, 0.125, ((1, 16),))
    encoder_bias = jnp.clip(-0.6 + 0.8 * jax.random.uniform(keys[5], (LATENTS,), jnp.float32) ** shard_levels(keys[5], (LATENTS,), ((0, 16),), -0.2, 0.2), -0.6, 0.2)
    decoder_weight = noise(keys[6], (LATENTS, D), SEG_LAT ** -0.5, 0.125, ((0, 16),))
    decoder_bias = noise(keys[7], (D,), 0.3, 1.5, (), jnp.float32)
    segment_sizes = draw_segment_sizes(jax.random.fold_in(keys[9], 71), 0)
    return {"activations": activations, "gate_weight": gate_weight, "up_weight": up_weight, "down_weight": down_weight, "encoder_weight": encoder_weight, "encoder_bias": encoder_bias, "decoder_weight": decoder_weight, "decoder_bias": decoder_bias, "segment_sizes": segment_sizes}


def reference(activations, gate_weight, up_weight, down_weight, encoder_weight, encoder_bias, decoder_weight, decoder_bias, segment_sizes):
    gate = jnp.dot(activations, gate_weight, preferred_element_type=jnp.float32)
    up_proj = jnp.dot(activations, up_weight, preferred_element_type=jnp.float32)
    hidden = (jax.nn.gelu(gate, approximate=True) * up_proj).astype(jnp.bfloat16)
    mlp_out = jnp.dot(hidden, down_weight, preferred_element_type=jnp.float32).astype(jnp.bfloat16)
    mlp_float = mlp_out.astype(jnp.float32)
    centered = (mlp_float - decoder_bias).astype(jnp.bfloat16)
    scale = 1.0 / math.sqrt(TOKENS)
    positions = jnp.arange(SEG_LAT, dtype=jnp.int32)
    running = jnp.zeros(mlp_float.shape, jnp.float32)
    code_list, slope_list, error_list, mse_list = ([], [], [], [])
    for segment in range(NSEG):
        first_latent = segment * SEG_LAT
        pre_act = jnp.dot(centered, encoder_weight[:, first_latent:first_latent + SEG_LAT], preferred_element_type=jnp.float32) + encoder_bias[first_latent:first_latent + SEG_LAT]
        live_mask = positions < segment_sizes[segment]
        codes = jnp.where(live_mask, jax.nn.softplus(10.0 * pre_act) / 10.0, 0.0).astype(jnp.bfloat16)
        slope = jnp.where(live_mask, jax.nn.sigmoid(10.0 * pre_act), 0.0)
        running = running + jnp.dot(codes, decoder_weight[first_latent:first_latent + SEG_LAT], preferred_element_type=jnp.float32)
        errors = decoder_bias + running - mlp_float
        code_list.append(codes)
        slope_list.append(slope)
        error_list.append(errors)
        mse_list.append(jnp.sum(errors * errors) / (TOKENS * D))
    later = jnp.zeros(mlp_float.shape, jnp.float32)
    encoder_parts = [None] * NSEG
    decoder_parts = [None] * NSEG
    for segment in reversed(range(NSEG)):
        first_latent = segment * SEG_LAT
        later = later + error_list[segment]
        back = (later * scale).astype(jnp.bfloat16)
        decoder_parts[segment] = jnp.dot(code_list[segment].T, back, preferred_element_type=jnp.float32)
        code_back = jnp.dot(back, decoder_weight[first_latent:first_latent + SEG_LAT].T, preferred_element_type=jnp.float32)
        code_grad = (code_back * slope_list[segment]).astype(jnp.bfloat16)
        encoder_parts[segment] = jnp.dot(centered.T, code_grad, preferred_element_type=jnp.float32)
    return (jnp.concatenate(encoder_parts, axis=1), jnp.concatenate(decoder_parts, axis=0), jnp.stack(mse_list))
```

```python
import functools
import math

import jax
import jax.numpy as jnp
from jax import lax
from jax.experimental import pallas as pl
from jax.experimental.pallas import tpu as pltpu
from jax.sharding import PartitionSpec as P

MESH = pl.DeviceIdType.MESH
F32 = jnp.float32
BF16 = jnp.bfloat16
TILE = 32
VMEM_BYTES = 52 * 1024 * 1024


def carried_in(value, axis, join, neutral, backward):
    count, mine = (lax.axis_size(axis), lax.axis_index(axis))
    pieces = lax.all_gather(value, axis)
    if backward:
        pieces = pieces[::-1]
        mine = count - 1 - mine
    subtotal = jnp.full_like(value, 0) + jnp.asarray(neutral, value.dtype)

    def hop(position, subtotal):
        longer = join(subtotal, pieces[position])
        return jnp.where(position < mine, longer, subtotal)

    return lax.fori_loop(0, count - 1, hop, subtotal)


def plain(
    activations,
    gate_weight,
    up_weight,
    down_weight,
    encoder_weight,
    encoder_bias,
    decoder_weight,
    decoder_bias,
    segment_sizes,
):
    shard_index = lax.axis_index("shard")
    segment_index = lax.axis_index("seg")
    group_index = lax.axis_index("tok")
    tok_rows = activations.shape[0]
    width_slice = activations.shape[1]
    gate_part = jnp.dot(activations, gate_weight, preferred_element_type=jnp.float32)
    up_part = jnp.dot(activations, up_weight, preferred_element_type=jnp.float32)
    gate_total, up_total = lax.psum((gate_part, up_part), "shard")
    hidden = (jax.nn.gelu(gate_total, approximate=True) * up_total).astype(jnp.bfloat16)
    down_part = jnp.dot(hidden, down_weight, preferred_element_type=jnp.float32)
    mlp_slice = lax.psum(down_part, "seg").astype(jnp.bfloat16)
    mlp_full = lax.all_gather(mlp_slice, "shard", axis=1, tiled=True)
    width = mlp_full.shape[1]
    groups = lax.axis_size("tok")
    tokens_all = tok_rows * groups
    half_width = width // groups
    mlp_float = mlp_full.astype(jnp.float32)
    centered = (mlp_float - decoder_bias).astype(jnp.bfloat16)
    lat_count = encoder_weight.shape[1]
    segment_total = segment_sizes.shape[0]
    size_here = jnp.sum(jnp.where(jnp.arange(segment_total) == segment_index, segment_sizes, 0))
    latent_index = shard_index * lat_count + jnp.arange(lat_count)
    live_mask = latent_index < size_here
    pre_act = jnp.dot(centered, encoder_weight, preferred_element_type=jnp.float32) + encoder_bias
    latent_codes = jnp.where(live_mask, jax.nn.softplus(10.0 * pre_act) / 10.0, 0.0).astype(
        jnp.bfloat16
    )
    slope = jnp.where(live_mask, jax.nn.sigmoid(10.0 * pre_act), 0.0)
    codes_all = lax.all_gather(latent_codes, "tok", axis=0, tiled=True)
    centered_all = lax.all_to_all(centered, "tok", split_axis=1, concat_axis=0, tiled=True)
    columns = decoder_weight
    my_part = lax.psum_scatter(
        lax.dot_general(
            columns, latent_codes, (((0,), (1,)), ((), ())), preferred_element_type=jnp.float32
        ),
        "shard",
        scatter_dimension=0,
        tiled=True,
    )
    column_start = shard_index * width_slice
    target = lax.dynamic_slice_in_dim(mlp_float, column_start, width_slice, 1).T
    bias_slice = lax.dynamic_slice_in_dim(decoder_bias, column_start, width_slice, 0)[:, None]
    blank = jnp.zeros_like(my_part)
    earlier = carried_in(my_part, "seg", jnp.add, blank, False)
    errors = bias_slice + (earlier + my_part) - target
    total_square = lax.psum(jnp.sum(errors * errors), ("shard", "tok"))
    prefix_mse = (total_square / (tokens_all * width)).reshape(1)
    later = carried_in(errors, "seg", jnp.add, blank, True)
    back = ((later + errors) * (1.0 / math.sqrt(tokens_all))).astype(jnp.bfloat16)
    back_all = lax.all_gather(back, "tok", axis=1, tiled=True)
    piece = lax.all_gather(back_all, "shard", axis=0, tiled=True)
    columns = decoder_weight
    own_piece = lax.dynamic_slice_in_dim(piece, group_index * tok_rows, tok_rows, 1)
    code_acc = lax.dot_general(
        own_piece, columns, (((0,), (1,)), ((), ())), preferred_element_type=jnp.float32
    )
    grad_piece = lax.dot_general(
        codes_all, piece, (((0,), (1,)), ((), ())), preferred_element_type=jnp.float32
    )
    code_grad = (code_acc * slope).astype(jnp.bfloat16)
    code_grad_all = lax.all_gather(code_grad, "tok", axis=0, tiled=True)
    grad_encoder = lax.dot_general(
        centered_all, code_grad_all, (((0,), (0,)), ((), ())), preferred_element_type=jnp.float32
    )
    grad_decoder = lax.dynamic_slice_in_dim(grad_piece, group_index * half_width, half_width, 1)
    return (grad_encoder, grad_decoder, prefix_mse)


def send(src, dst, send_sem, recv_sem, **place):
    return pltpu.make_async_remote_copy(
        src_ref=src,
        dst_ref=dst,
        send_sem=send_sem,
        recv_sem=recv_sem,
        device_id=place,
        device_id_type=MESH,
    )


def greet(peers):
    barrier = pltpu.get_barrier_semaphore()
    for place in peers:
        pl.semaphore_signal(barrier, inc=1, device_id=place, device_id_type=MESH)
    pl.semaphore_wait(barrier, len(peers))


def by_rows(total, body):
    def step(i, carry):
        body(i * TILE)
        return carry

    lax.fori_loop(0, total // TILE, step, 0)


def tile_at(first):
    return pl.ds(pl.multiple_of(first, TILE), TILE)


def span(index, size):
    return pl.ds(pl.multiple_of(index * size, 128 if size % 128 == 0 else 32), size)


def dot(a, b):
    return jnp.dot(a, b, preferred_element_type=F32)


def dot_t(a, b):
    return lax.dot_general(a, b, (((1,), (1,)), ((), ())), preferred_element_type=F32)


def gelu_tanh(x):
    return x * (0.5 * (1.0 + jnp.tanh(math.sqrt(2.0 / math.pi) * (x + 0.044715 * (x * x * x)))))


def mlp_kernel(
    n, outer, act, wg, wu, wd, out,
    send_a, recv_a, gate, up, hid, down, got, half, far,
    sa, ra, sb, rb, sc, rc, sz, rz, sd, rd, se, re,
):
    me, sg = lax.axis_index("shard"), lax.axis_index("seg")
    core, group = sg % 2, sg // 2
    twin = sg + 1 - 2 * core
    chunk = wg.shape[1] // n
    width = wd.shape[1]
    rows = act.shape[0]
    part = rows // 2
    greet(
        [{"shard": (me + d) % n} for d in range(1, n)]
        + [{"seg": twin}]
        + [{"seg": ((group + d) % outer) * 2 + core} for d in range(1, outer)]
    )

    def to_peer(d, carry):
        p = (me + d) % n
        send_a[d - 1, :, :chunk] = dot(act[...], wg[:, span(p, chunk)]).astype(BF16)
        send_a[d - 1, :, chunk:] = dot(act[...], wu[:, span(p, chunk)]).astype(BF16)
        send(send_a.at[d - 1], recv_a.at[d - 1], sa.at[d - 1], ra.at[d - 1], shard=p).start()
        return carry

    lax.fori_loop(1, n, to_peer, 0)
    gate[...] = dot(act[...], wg[:, span(me, chunk)])
    up[...] = dot(act[...], wu[:, span(me, chunk)])
    for d in range(1, n):
        send(
            send_a.at[d - 1], recv_a.at[d - 1], sa.at[d - 1], ra.at[d - 1], shard=(me + d) % n
        ).wait()

    def hidden_rows(first):
        r = tile_at(first)
        g, u = gate[r, :], up[r, :]
        for d in range(n - 1):
            g = g + recv_a[d, r, :chunk].astype(F32)
            u = u + recv_a[d, r, chunk:].astype(F32)
        hid[0, r, :] = (gelu_tanh(g) * u).astype(BF16)

    by_rows(rows, hidden_rows)

    def hid_copy(d):
        return send(hid.at[0], hid.at[d], sb.at[d - 1], rb.at[d - 1], shard=(me + d) % n)

    for d in range(1, n):
        hid_copy(d).start()
    down[...] = dot(hid[0], wd[span(me, chunk), :])

    def from_peer(d, carry):
        hid_copy(d).wait_recv()
        down[...] += dot(hid[d], wd[span((me + n - d) % n, chunk), :])
        return carry

    lax.fori_loop(1, n, from_peer, 0)

    core_copy = send(down.at[span(1 - core, part), :], got, sc.at[0], rc.at[0], seg=twin)
    core_copy.start()
    core_copy.wait()

    def half_rows(first):
        r = tile_at(first)
        half[r, :] = (down[tile_at(core * part + first), :] + got[r, :]).astype(BF16)

    by_rows(part, half_rows)

    def far_copy(d):
        to = ((group + d) % outer) * 2 + core
        return send(half, far.at[d - 1], sz.at[d - 1], rz.at[d - 1], seg=to)

    for d in range(1, outer):
        far_copy(d).start()
    for d in range(1, outer):
        far_copy(d).wait()

    def out_rows(first):
        r = tile_at(first)
        total = half[r, :].astype(F32)
        for d in range(outer - 1):
            total = total + far[d, r, :].astype(F32)
        out[tile_at(core * part + first), span(me, width)] = total.astype(BF16)

    by_rows(part, out_rows)

    def block(c, s):
        return out.at[span(c, part), span(s, width)]

    def shard_copy(d, s):
        return send(block(core, s), block(core, s), sd.at[d - 1], rd.at[d - 1], shard=(me + d) % n)

    def twin_copy(d, c, s):
        return send(block(c, s), block(c, s), se.at[d], re.at[d], seg=twin)

    for d in range(1, n):
        shard_copy(d, me).start()
    twin_copy(0, core, me).start()
    for d in range(1, n):
        s = (me + n - d) % n
        shard_copy(d, s).wait_recv()
        twin_copy(d, core, s).start()
    for d in range(n):
        twin_copy(d, 1 - core, (me + n - d) % n).wait_recv()
    for d in range(1, n):
        hid_copy(d).wait_send()
        shard_copy(d, me).wait_send()
    for d in range(n):
        twin_copy(d, core, (me + n - d) % n).wait_send()


def sae_kernel(
    n, outer, scale, count, mlp, enc, enc_bias, dec, dec_bias, live,
    cen_out, code_out, back_out, grad_out, mse_out,
    cen, slope, send_e, recv_e, mine, other, payload, far, back, acc, square, square_in, square_tok,
    su, ru, sv, rv, sk, rk, sa, ra, sp, rp, sz, rz, sf, rf, sb, rb, st, rt, sg_, rg_, sm, rm, sn, rn,
):
    me, sg, tok = lax.axis_index("shard"), lax.axis_index("seg"), lax.axis_index("tok")
    core, group = sg % 2, sg // 2
    twin = sg + 1 - 2 * core
    peer = 1 - tok
    segments = outer * 2
    rows, depth = mlp.shape
    width = depth // n
    half_width = depth // 2
    part = rows // 2
    per_half = n // 2
    greet(
        [{"shard": (me + d) % n} for d in range(1, n)]
        + [{"seg": twin}, {"tok": peer}]
        + [{"seg": ((group + d) % outer) * 2 + core} for d in range(1, outer)]
    )

    def center_rows(first):
        r = tile_at(first)
        cen[r, :] = (mlp[r, :].astype(F32) - dec_bias[...]).astype(BF16)
        cen_out[0, r, :] = cen[r, span(tok, half_width)]

    by_rows(rows, center_rows)

    def cen_tok():
        return send(
            cen.at[span(core, part), span(peer, half_width)],
            cen_out.at[1, span(core, part), :],
            su.at[0], ru.at[0], tok=peer,
        )

    def cen_twin(c):
        piece = cen_out.at[1, span(c, part), :]
        return send(piece, piece, sv.at[0], rv.at[0], seg=twin)

    cen_tok().start()
    latents = enc.shape[1]
    step = 256 if latents % 256 == 0 else 128

    def encode(i, carry):
        c = span(i, step)
        pre = 10.0 * (dot(cen[...], enc[:, c]) + enc_bias[:, c])
        on = live[:, c] > 0.0
        soft = jnp.maximum(pre, 0.0) + jnp.log1p(jnp.exp(-jnp.abs(pre)))
        code_out[0, :, c] = jnp.where(on, soft / 10.0, 0.0).astype(BF16)
        slope[:, c] = jnp.where(on, jax.nn.sigmoid(pre), 0.0)
        return carry

    lax.fori_loop(0, latents // step, encode, 0)
    code_copy = send(code_out.at[0], code_out.at[1], sk.at[0], rk.at[0], tok=peer)

    def to_peer(d, carry):
        p = (me + d) % n
        send_e[d - 1] = dot(code_out[0], dec[:, span(p, width)]).astype(BF16)
        send(send_e.at[d - 1], recv_e.at[d - 1], sa.at[d - 1], ra.at[d - 1], shard=p).start()
        return carry

    lax.fori_loop(1, n, to_peer, 0)
    code_copy.start()
    mine[...] = dot(code_out[0], dec[:, span(me, width)])
    cen_tok().wait_recv()
    cen_twin(core).start()
    for d in range(1, n):
        send(
            send_e.at[d - 1], recv_e.at[d - 1], sa.at[d - 1], ra.at[d - 1], shard=(me + d) % n
        ).wait()

    def mine_rows(first):
        r = tile_at(first)
        total = mine[r, :]
        for d in range(n - 1):
            total = total + recv_e[d, r, :].astype(F32)
        mine[r, :] = total

    by_rows(rows, mine_rows)
    twin_part = send(mine, other, sp.at[0], rp.at[0], seg=twin)
    twin_part.start()
    twin_part.wait()

    def far_copy(d):
        to = ((group + d) % outer) * 2 + core
        piece = far.at[d - 1, span(core, part), :]
        return send(payload.at[d - 1], piece, sz.at[d - 1], rz.at[d - 1], seg=to)

    def far_twin(d, c):
        piece = far.at[d - 1, span(c, part), :]
        return send(piece, piece, sf.at[d - 1], rf.at[d - 1], seg=twin)

    for d in range(1, outer):
        later = (group + d) % outer > group
        weight_mine = jnp.where(later, 1, segments - sg).astype(F32)
        weight_other = jnp.where(later, 1, segments - twin).astype(F32)

        def payload_rows(first, d=d, weight_mine=weight_mine, weight_other=weight_other):
            q = tile_at(core * part + first)
            payload[d - 1, tile_at(first), :] = (
                weight_mine * mine[q, :] + weight_other * other[q, :]
            ).astype(BF16)

        by_rows(part, payload_rows)
        far_copy(d).start()
    for d in range(1, outer):
        far_copy(d).wait_recv()
        far_twin(d, core).start()
    for d in range(1, outer):
        far_twin(d, 1 - core).wait_recv()

    ahead = (segments - sg).astype(F32)
    other_error = core.astype(F32)
    other_back = (segments - sg - 1 + core).astype(F32)
    square[...] = jnp.zeros_like(square)
    bias_here = dec_bias[:, span(me, width)]

    def error_rows(first):
        r = tile_at(first)
        here, there = mine[r, :], other[r, :]
        base = bias_here - mlp[r, span(me, width)].astype(F32)
        after = jnp.zeros_like(here)
        for d in range(1, outer):
            before = ((group + outer - d) % outer < group).astype(F32)
            arrived = far[d - 1, r, :].astype(F32)
            base = base + before * arrived
            after = after + (1.0 - before) * arrived
        error = base + other_error * there + here
        square[...] += error * error
        total = ahead * (base + here) + other_back * there + after
        back[r, span(me, width)] = (total * scale).astype(BF16)

    by_rows(rows, error_rows)

    def back_block(s):
        return back.at[:, span(s, width)]

    def back_copy(d, s):
        return send(back_block(s), back_block(s), sb.at[d - 1], rb.at[d - 1], shard=(me + d) % n)

    def back_tok(s, q):
        return send(
            back_block(s), back_out.at[1, :, span(q, width)], st.at[q], rt.at[q], tok=peer
        )

    def pass_on(s):
        @pl.when(s // per_half == peer)
        def _():
            back_tok(s, s % per_half).start()

    for d in range(1, n):
        back_copy(d, me).start()
    pass_on(me)
    square_sum = jnp.sum(square[...]) / count
    square_in[0] = jnp.full(square_in.shape[1:], square_sum, F32)

    def square_copy(d):
        return send(
            square_in.at[0], square_in.at[d], sm.at[d - 1], rm.at[d - 1], shard=(me + d) % n
        )

    for d in range(1, n):
        square_copy(d).start()
    acc[...] = dot_t(back[:, span(me, width)], dec[:, span(me, width)])

    def back_in(d, carry):
        s = (me + n - d) % n
        back_copy(d, s).wait_recv()
        pass_on(s)
        acc[...] += dot_t(back[:, span(s, width)], dec[:, span(s, width)])
        return carry

    lax.fori_loop(1, n, back_in, 0)

    def grad_rows(first):
        r = tile_at(first)
        grad_out[0, r, :] = (acc[r, :] * slope[r, :]).astype(BF16)

    by_rows(rows, grad_rows)
    grad_copy = send(grad_out.at[0], grad_out.at[1], sg_.at[0], rg_.at[0], tok=peer)
    grad_copy.start()
    for d in range(1, n):
        square_copy(d).wait()
    total = square_in[0]
    for d in range(1, n):
        total = total + square_in[d]
    square_tok[0] = total
    tok_copy = send(square_tok.at[0], square_tok.at[1], sn.at[0], rn.at[0], tok=peer)
    tok_copy.start()

    def own_back(first):
        r = tile_at(first)
        back_out[0, r, :] = back[r, span(tok, half_width)]

    by_rows(rows, own_back)
    tok_copy.wait()
    mse_out[...] = square_tok[0] + square_tok[1]
    code_copy.wait()
    cen_tok().wait_send()
    cen_twin(1 - core).wait_recv()
    cen_twin(core).wait_send()
    for d in range(1, outer):
        far_copy(d).wait_send()
        far_twin(d, core).wait_send()
    for d in range(1, n):
        back_copy(d, me).wait_send()
    for q in range(per_half):
        back_tok(peer * per_half + q, q).wait()
    grad_copy.wait()


def vmem(count):
    return [pl.BlockSpec(memory_space=pltpu.VMEM)] * count


def sems(*sizes):
    found = []
    for size in sizes:
        found += [pltpu.SemaphoreType.DMA((max(size, 1),))] * 2
    return found


def params(number):
    return pltpu.CompilerParams(
        collective_id=number, has_side_effects=True, vmem_limit_bytes=VMEM_BYTES
    )


def mlp_call(activations, gate_weight, up_weight, down_weight):
    n, outer = lax.axis_size("shard"), lax.axis_size("seg") // 2
    rows = activations.shape[0]
    chunk, width = gate_weight.shape[1] // n, down_weight.shape[1]
    part, far = rows // 2, max(outer - 1, 1)
    return pl.pallas_call(
        functools.partial(mlp_kernel, n, outer),
        out_shape=jax.ShapeDtypeStruct((rows, width * n), BF16),
        in_specs=vmem(4),
        out_specs=vmem(1)[0],
        scratch_shapes=[
            pltpu.VMEM((n - 1, rows, 2 * chunk), BF16),
            pltpu.VMEM((n - 1, rows, 2 * chunk), BF16),
            pltpu.VMEM((rows, chunk), F32),
            pltpu.VMEM((rows, chunk), F32),
            pltpu.VMEM((n, rows, chunk), BF16),
            pltpu.VMEM((rows, width), F32),
            pltpu.VMEM((part, width), F32),
            pltpu.VMEM((part, width), BF16),
            pltpu.VMEM((far, part, width), BF16),
            *sems(n - 1, n - 1, 1, outer - 1, n - 1, n),
        ],
        compiler_params=params(0),
        name="mlp",
    )(activations, gate_weight, up_weight, down_weight)


def sae_call(mlp, enc, enc_bias, dec, dec_bias, live):
    n, outer = lax.axis_size("shard"), lax.axis_size("seg") // 2
    rows, depth = mlp.shape
    width, latents = depth // n, enc.shape[1]
    part, far, half = rows // 2, max(outer - 1, 1), depth // 2
    tokens = rows * lax.axis_size("tok")
    shape = jax.ShapeDtypeStruct
    return pl.pallas_call(
        functools.partial(sae_kernel, n, outer, 1.0 / math.sqrt(tokens), tokens * depth),
        out_shape=(
            shape((2, rows, half), BF16),
            shape((2, rows, latents), BF16),
            shape((2, rows, half), BF16),
            shape((2, rows, latents), BF16),
            shape((8, 128), F32),
        ),
        in_specs=vmem(6),
        out_specs=tuple(vmem(5)),
        scratch_shapes=[
            pltpu.VMEM((rows, depth), BF16),
            pltpu.VMEM((rows, latents), F32),
            pltpu.VMEM((n - 1, rows, width), BF16),
            pltpu.VMEM((n - 1, rows, width), BF16),
            pltpu.VMEM((rows, width), F32),
            pltpu.VMEM((rows, width), F32),
            pltpu.VMEM((far, part, width), BF16),
            pltpu.VMEM((far, rows, width), BF16),
            pltpu.VMEM((rows, depth), BF16),
            pltpu.VMEM((rows, latents), F32),
            pltpu.VMEM((TILE, width), F32),
            pltpu.VMEM((n, 8, 128), F32),
            pltpu.VMEM((2, 8, 128), F32),
            *sems(1, 1, 1, n - 1, 1, outer - 1, outer - 1, n - 1, n // 2, 1, n - 1, 1),
        ],
        compiler_params=params(1),
        name="sae",
    )(mlp, enc, enc_bias, dec, dec_bias, live)


def fits(activations, gate_weight, encoder_weight):
    n, segs, toks = lax.axis_size("shard"), lax.axis_size("seg"), lax.axis_size("tok")
    rows, width = activations.shape
    lanes = (width, gate_weight.shape[1] // n, encoder_weight.shape[1])
    return (
        toks == 2
        and n % 2 == 0
        and segs % 2 == 0
        and rows % (2 * TILE) == 0
        and all(size % 128 == 0 for size in lanes)
    )


def local(
    activations,
    gate_weight,
    up_weight,
    down_weight,
    encoder_weight,
    encoder_bias,
    decoder_weight,
    decoder_bias,
    segment_sizes,
):
    if not fits(activations, gate_weight, encoder_weight):
        return plain(
            activations,
            gate_weight,
            up_weight,
            down_weight,
            encoder_weight,
            encoder_bias,
            decoder_weight,
            decoder_bias,
            segment_sizes,
        )
    latents = encoder_weight.shape[1]
    here = jnp.arange(segment_sizes.shape[0]) == lax.axis_index("seg")
    size_here = jnp.sum(jnp.where(here, segment_sizes, 0))
    index = lax.axis_index("shard") * latents + jnp.arange(latents)
    live = (index < size_here).astype(F32)[None, :]
    mlp = mlp_call(activations, gate_weight, up_weight, down_weight)
    cen, codes, back, code_grad, mse = sae_call(
        mlp, encoder_weight, encoder_bias[None, :], decoder_weight, decoder_bias[None, :], live
    )

    def over_tokens(a, b):
        a, b = (value.reshape(-1, value.shape[2]) for value in (a, b))
        return lax.dot_general(a, b, (((0,), (0,)), ((), ())), preferred_element_type=F32)

    return over_tokens(cen, code_grad), over_tokens(codes, back), mse[0, :1]


def solution(mesh):
    in_specs = (
        P("tok", "shard"),
        P("shard", "seg"),
        P("shard", "seg"),
        P("seg", "shard"),
        P(None, ("seg", "shard")),
        P(("seg", "shard")),
        P(("seg", "shard"), None),
        P(),
        P(),
    )
    out_specs = (P("tok", ("seg", "shard")), P(("seg", "shard"), "tok"), P("seg"))
    return jax.shard_map(local, mesh=mesh, in_specs=in_specs, out_specs=out_specs, check_vma=False)
```

```python
import functools
import math

import jax
import jax.numpy as jnp
from jax import lax
from jax.experimental import pallas as pl
from jax.experimental.pallas import tpu as pltpu
from jax.sharding import PartitionSpec as P

MESH = pl.DeviceIdType.MESH
F32 = jnp.float32
BF16 = jnp.bfloat16
TILE = 32
VMEM_BYTES = 52 * 1024 * 1024


def carried_in(value, axis, join, neutral, backward):
    count, mine = (lax.axis_size(axis), lax.axis_index(axis))
    pieces = lax.all_gather(value, axis)
    if backward:
        pieces = pieces[::-1]
        mine = count - 1 - mine
    subtotal = jnp.full_like(value, 0) + jnp.asarray(neutral, value.dtype)

    def hop(position, subtotal):
        longer = join(subtotal, pieces[position])
        return jnp.where(position < mine, longer, subtotal)

    return lax.fori_loop(0, count - 1, hop, subtotal)


def plain(
    activations,
    gate_weight,
    up_weight,
    down_weight,
    encoder_weight,
    encoder_bias,
    decoder_weight,
    decoder_bias,
    segment_sizes,
):
    shard_index = lax.axis_index("shard")
    segment_index = lax.axis_index("seg")
    group_index = lax.axis_index("tok")
    tok_rows = activations.shape[0]
    width_slice = activations.shape[1]
    gate_part = jnp.dot(activations, gate_weight, preferred_element_type=jnp.float32)
    up_part = jnp.dot(activations, up_weight, preferred_element_type=jnp.float32)
    gate_total, up_total = lax.psum((gate_part, up_part), "shard")
    hidden = (jax.nn.gelu(gate_total, approximate=True) * up_total).astype(jnp.bfloat16)
    down_part = jnp.dot(hidden, down_weight, preferred_element_type=jnp.float32)
    mlp_slice = lax.psum(down_part, "seg").astype(jnp.bfloat16)
    mlp_full = lax.all_gather(mlp_slice, "shard", axis=1, tiled=True)
    width = mlp_full.shape[1]
    groups = lax.axis_size("tok")
    tokens_all = tok_rows * groups
    half_width = width // groups
    mlp_float = mlp_full.astype(jnp.float32)
    centered = (mlp_float - decoder_bias).astype(jnp.bfloat16)
    lat_count = encoder_weight.shape[1]
    segment_total = segment_sizes.shape[0]
    size_here = jnp.sum(jnp.where(jnp.arange(segment_total) == segment_index, segment_sizes, 0))
    latent_index = shard_index * lat_count + jnp.arange(lat_count)
    live_mask = latent_index < size_here
    pre_act = jnp.dot(centered, encoder_weight, preferred_element_type=jnp.float32) + encoder_bias
    latent_codes = jnp.where(live_mask, jax.nn.softplus(10.0 * pre_act) / 10.0, 0.0).astype(
        jnp.bfloat16
    )
    slope = jnp.where(live_mask, jax.nn.sigmoid(10.0 * pre_act), 0.0)
    codes_all = lax.all_gather(latent_codes, "tok", axis=0, tiled=True)
    centered_all = lax.all_to_all(centered, "tok", split_axis=1, concat_axis=0, tiled=True)
    columns = decoder_weight
    my_part = lax.psum_scatter(
        lax.dot_general(
            columns, latent_codes, (((0,), (1,)), ((), ())), preferred_element_type=jnp.float32
        ),
        "shard",
        scatter_dimension=0,
        tiled=True,
    )
    column_start = shard_index * width_slice
    target = lax.dynamic_slice_in_dim(mlp_float, column_start, width_slice, 1).T
    bias_slice = lax.dynamic_slice_in_dim(decoder_bias, column_start, width_slice, 0)[:, None]
    blank = jnp.zeros_like(my_part)
    earlier = carried_in(my_part, "seg", jnp.add, blank, False)
    errors = bias_slice + (earlier + my_part) - target
    total_square = lax.psum(jnp.sum(errors * errors), ("shard", "tok"))
    prefix_mse = (total_square / (tokens_all * width)).reshape(1)
    later = carried_in(errors, "seg", jnp.add, blank, True)
    back = ((later + errors) * (1.0 / math.sqrt(tokens_all))).astype(jnp.bfloat16)
    back_all = lax.all_gather(back, "tok", axis=1, tiled=True)
    piece = lax.all_gather(back_all, "shard", axis=0, tiled=True)
    columns = decoder_weight
    own_piece = lax.dynamic_slice_in_dim(piece, group_index * tok_rows, tok_rows, 1)
    code_acc = lax.dot_general(
        own_piece, columns, (((0,), (1,)), ((), ())), preferred_element_type=jnp.float32
    )
    grad_piece = lax.dot_general(
        codes_all, piece, (((0,), (1,)), ((), ())), preferred_element_type=jnp.float32
    )
    code_grad = (code_acc * slope).astype(jnp.bfloat16)
    code_grad_all = lax.all_gather(code_grad, "tok", axis=0, tiled=True)
    grad_encoder = lax.dot_general(
        centered_all, code_grad_all, (((0,), (0,)), ((), ())), preferred_element_type=jnp.float32
    )
    grad_decoder = lax.dynamic_slice_in_dim(grad_piece, group_index * half_width, half_width, 1)
    return (grad_encoder, grad_decoder, prefix_mse)


def send(src, dst, send_sem, recv_sem, **place):
    return pltpu.make_async_remote_copy(
        src_ref=src,
        dst_ref=dst,
        send_sem=send_sem,
        recv_sem=recv_sem,
        device_id=place,
        device_id_type=MESH,
    )


def greet(peers):
    barrier = pltpu.get_barrier_semaphore()
    for place in peers:
        pl.semaphore_signal(barrier, inc=1, device_id=place, device_id_type=MESH)
    pl.semaphore_wait(barrier, len(peers))


def by_rows(total, body):
    def step(i, carry):
        body(i * TILE)
        return carry

    lax.fori_loop(0, total // TILE, step, 0)


def tile_at(first):
    return pl.ds(pl.multiple_of(first, TILE), TILE)


def span(index, size):
    return pl.ds(pl.multiple_of(index * size, 128 if size % 128 == 0 else 32), size)


def dot(a, b):
    return jnp.dot(a, b, preferred_element_type=F32)


def dot_t(a, b):
    return lax.dot_general(a, b, (((1,), (1,)), ((), ())), preferred_element_type=F32)


def gelu_tanh(x):
    return x * (0.5 * (1.0 + jnp.tanh(math.sqrt(2.0 / math.pi) * (x + 0.044715 * (x * x * x)))))


class Links:
    def __init__(self, send_sems, recv_sems):
        self.sems, self.copies = (send_sems, recv_sems), {}

    def start(self, number, src, dst, **place):
        sent, got = (group.at[number] for group in self.sems)
        self.copies[number] = send(src, dst, sent, got, **place)
        self.copies[number].start()

    def arrived(self, *numbers):
        for number in numbers:
            self.copies[number].wait_recv()

    def finish(self):
        for copy in self.copies.values():
            copy.wait_send()


def square_of(me):
    x = me + 1 - 2 * (me % 2)
    y = (me + 2) % 4
    return x, y, (x + 2) % 4


def scatter_start(links, base, fill, square, half, bufs):
    x, y, corner = square
    to_corner, to_x, to_y, via_x, via_y, from_x, from_y = bufs
    top, low = pl.ds(0, half), pl.ds(half, half)
    fill(to_corner, corner)
    links.start(base, to_corner.at[top, :], via_x, shard=x)
    links.start(base + 1, to_corner.at[low, :], via_y, shard=y)
    fill(to_x, x)
    links.start(base + 2, to_x.at[top, :], from_x.at[top, :], shard=x)
    fill(to_y, y)
    links.start(base + 3, to_y.at[low, :], from_y.at[low, :], shard=y)


def scatter_forward(links, base, square, half, bufs):
    x, y, _ = square
    _, to_x, to_y, via_x, via_y, from_x, from_y = bufs
    top, low = pl.ds(0, half), pl.ds(half, half)

    def add_top(first):
        r = tile_at(first)
        to_y[r, :] = (to_y[r, :].astype(F32) + via_x[r, :].astype(F32)).astype(BF16)

    def add_low(first):
        r, q = tile_at(first), tile_at(half + first)
        to_x[q, :] = (to_x[q, :].astype(F32) + via_y[r, :].astype(F32)).astype(BF16)

    links.arrived(base)
    by_rows(half, add_top)
    links.start(base + 4, to_y.at[top, :], from_y.at[top, :], shard=y)
    links.arrived(base + 1)
    by_rows(half, add_low)
    links.start(base + 5, to_x.at[low, :], from_x.at[low, :], shard=x)


def scatter_wait(links, base):
    links.arrived(base + 2, base + 3, base + 4, base + 5)


def gather_start(links, base, block, me, square):
    x, y, _ = square
    links.start(base, block(me), block(me), shard=x)
    links.start(base + 1, block(me), block(me), shard=y)


def gather_pass_x(links, base, block, square):
    x, y, _ = square
    links.arrived(base)
    links.start(base + 2, block(x, 0), block(x, 0), shard=y)


def gather_pass_y(links, base, block, square):
    x, y, _ = square
    links.arrived(base + 1)
    links.start(base + 3, block(y, 1), block(y, 1), shard=x)


def mlp_kernel(
    outer, act, wg, wu, wd, out,
    to_corner, to_x, to_y, via_x, via_y, from_x, from_y,
    gate, up, hid, down, got, half, far, sent, arrived,
):
    me, sg = lax.axis_index("shard"), lax.axis_index("seg")
    core, group = sg % 2, sg // 2
    twin = sg + 1 - 2 * core
    square = square_of(me)
    x, y, corner = square
    chunk = wg.shape[1] // 4
    width = wd.shape[1]
    rows = act.shape[0] // 2
    part = rows // 2
    small = part // 2
    links = Links(sent, arrived)
    stride = 19 + outer - 1
    greet(
        [{"shard": x}, {"shard": y}, {"seg": twin}]
        + [{"seg": ((group + d) % outer) * 2 + core} for d in range(1, outer)]
    )

    def bufs(t):
        return [b.at[t] for b in (to_corner, to_x, to_y, via_x, via_y, from_x, from_y)]

    def tokens(t):
        return act[t * rows : (t + 1) * rows, :]

    def partial_start(t):
        def fill(ref, p):
            ref[:, :chunk] = dot(tokens(t), wg[:, span(p, chunk)]).astype(BF16)
            ref[:, chunk:] = dot(tokens(t), wu[:, span(p, chunk)]).astype(BF16)

        scatter_start(links, t * stride, fill, square, part, bufs(t))

    def partial_forward(t):
        scatter_forward(links, t * stride, square, part, bufs(t))

    def partial_own(t):
        gate[t] = dot(tokens(t), wg[:, span(me, chunk)])
        up[t] = dot(tokens(t), wu[:, span(me, chunk)])

    def hid_block(t):
        def block(s, k=None):
            r = pl.ds(0, rows) if k is None else pl.ds(k * part, part)
            return hid.at[t, s, r, :]

        return block

    def hidden_start(t):
        scatter_wait(links, t * stride)

        def hidden_rows(first):
            r = tile_at(first)
            g = gate[t, r, :] + from_x[t, r, :chunk].astype(F32) + from_y[t, r, :chunk].astype(F32)
            u = up[t, r, :] + from_x[t, r, chunk:].astype(F32) + from_y[t, r, chunk:].astype(F32)
            hid[t, me, r, :] = (gelu_tanh(g) * u).astype(BF16)

        by_rows(rows, hidden_rows)
        gather_start(links, t * stride + 6, hid_block(t), me, square)

    def hidden_forward(t):
        gather_pass_x(links, t * stride + 6, hid_block(t), square)
        gather_pass_y(links, t * stride + 6, hid_block(t), square)

    def term(t, s):
        return dot(hid[t, s], wd[span(s, chunk), :])

    def down_near(t):
        down[t] = term(t, me) + term(t, x) + term(t, y)

    def down_start(t):
        links.arrived(t * stride + 8, t * stride + 9)
        down[t] += term(t, corner)
        links.start(t * stride + 10, down.at[t, span(1 - core, part), :], got.at[t], seg=twin)

    def far_start(t):
        links.arrived(t * stride + 10)

        def half_rows(first):
            r = tile_at(first)
            half[t, r, :] = (down[t, tile_at(core * part + first), :] + got[t, r, :]).astype(BF16)

        by_rows(part, half_rows)
        for d in range(1, outer):
            to = ((group + d) % outer) * 2 + core
            links.start(t * stride + 18 + d, half.at[t], far.at[t, d - 1], seg=to)

    def out_block(t):
        def block(s, k=None):
            first = t * rows + core * part
            if k is None:
                r = pl.ds(pl.multiple_of(first, 32), part)
            else:
                r = pl.ds(pl.multiple_of(first + k * small, 16), small)
            return out.at[r, span(s, width)]

        return block

    def twin_start(t, number, s):
        piece = out_block(t)(s)
        links.start(t * stride + 15 + number, piece, piece, seg=twin)

    def out_start(t):
        for d in range(1, outer):
            links.arrived(t * stride + 18 + d)

        def out_rows(first):
            r = tile_at(first)
            total = half[t, r, :].astype(F32)
            for d in range(outer - 1):
                total = total + far[t, d, r, :].astype(F32)
            out[tile_at(t * rows + core * part + first), span(me, width)] = total.astype(BF16)

        by_rows(part, out_rows)
        gather_start(links, t * stride + 11, out_block(t), me, square)
        twin_start(t, 0, me)

    def out_forward(t):
        gather_pass_x(links, t * stride + 11, out_block(t), square)
        twin_start(t, 1, x)
        gather_pass_y(links, t * stride + 11, out_block(t), square)
        twin_start(t, 2, y)

    def out_last(t):
        links.arrived(t * stride + 13, t * stride + 14)
        twin_start(t, 3, corner)

    partial_start(0)
    partial_forward(0)
    partial_start(1)
    partial_own(0)
    hidden_start(0)
    partial_forward(1)
    partial_own(1)
    hidden_forward(0)
    down_near(0)
    hidden_start(1)
    down_start(0)
    far_start(0)
    hidden_forward(1)
    down_near(1)
    out_start(0)
    down_start(1)
    far_start(1)
    out_forward(0)
    out_last(0)
    out_start(1)
    out_forward(1)
    out_last(1)
    for t in range(2):
        links.arrived(*(t * stride + 15 + k for k in range(4)))
    links.finish()


def sae_kernel(
    outer, scale, count, mlp, enc, enc_bias, dec, dec_bias, live,
    cen_out, code_out, back_out, grad_out, mse_out,
    cen, slope, to_corner, to_x, to_y, via_x, via_y, from_x, from_y, mine, other, payload, far, back, acc, squares, square_in, square_tok,
    sent, arrived,
    su, ru, sv, rv, sk, rk, sp, rp, sz, rz, sf, rf, st, rt, sg_, rg_, sn, rn,
):
    me, sg, tok = lax.axis_index("shard"), lax.axis_index("seg"), lax.axis_index("tok")
    core, group = sg % 2, sg // 2
    twin = sg + 1 - 2 * core
    peer = 1 - tok
    square = square_of(me)
    x, y, corner = square
    links = Links(sent, arrived)
    n = 4
    segments = outer * 2
    rows, depth = mlp.shape
    width = depth // n
    half_width = depth // 2
    part = rows // 2
    per_half = n // 2
    greet(
        [{"shard": x}, {"shard": y}, {"seg": twin}, {"tok": peer}]
        + [{"seg": ((group + d) % outer) * 2 + core} for d in range(1, outer)]
    )

    def center_rows(first):
        r = tile_at(first)
        cen[r, :] = (mlp[r, :].astype(F32) - dec_bias[...]).astype(BF16)
        cen_out[0, r, :] = cen[r, span(tok, half_width)]

    by_rows(rows, center_rows)

    def cen_tok():
        return send(
            cen.at[span(core, part), span(peer, half_width)],
            cen_out.at[1, span(core, part), :],
            su.at[0], ru.at[0], tok=peer,
        )

    def cen_twin(c):
        piece = cen_out.at[1, span(c, part), :]
        return send(piece, piece, sv.at[0], rv.at[0], seg=twin)

    cen_tok().start()
    latents = enc.shape[1]
    step = 256 if latents % 256 == 0 else 128

    def encode(i, carry):
        c = span(i, step)
        pre = 10.0 * (dot(cen[...], enc[:, c]) + enc_bias[:, c])
        on = live[:, c] > 0.0
        soft = jnp.maximum(pre, 0.0) + jnp.log1p(jnp.exp(-jnp.abs(pre)))
        code_out[0, :, c] = jnp.where(on, soft / 10.0, 0.0).astype(BF16)
        slope[:, c] = jnp.where(on, jax.nn.sigmoid(pre), 0.0)
        return carry

    lax.fori_loop(0, latents // step, encode, 0)
    code_copy = send(code_out.at[0], code_out.at[1], sk.at[0], rk.at[0], tok=peer)

    bufs = (to_corner, to_x, to_y, via_x, via_y, from_x, from_y)

    def fill(ref, p):
        ref[...] = dot(code_out[0], dec[:, span(p, width)]).astype(BF16)

    scatter_start(links, 0, fill, square, part, bufs)
    code_copy.start()
    mine[...] = dot(code_out[0], dec[:, span(me, width)])
    scatter_forward(links, 0, square, part, bufs)
    cen_tok().wait_recv()
    cen_twin(core).start()
    scatter_wait(links, 0)

    def mine_rows(first):
        r = tile_at(first)
        mine[r, :] = mine[r, :] + from_x[r, :].astype(F32) + from_y[r, :].astype(F32)

    by_rows(rows, mine_rows)
    twin_part = send(mine, other, sp.at[0], rp.at[0], seg=twin)
    twin_part.start()
    twin_part.wait()

    def far_copy(d):
        to = ((group + d) % outer) * 2 + core
        piece = far.at[d - 1, span(core, part), :]
        return send(payload.at[d - 1], piece, sz.at[d - 1], rz.at[d - 1], seg=to)

    def far_twin(d, c):
        piece = far.at[d - 1, span(c, part), :]
        return send(piece, piece, sf.at[d - 1], rf.at[d - 1], seg=twin)

    for d in range(1, outer):
        later = (group + d) % outer > group
        weight_mine = jnp.where(later, 1, segments - sg).astype(F32)
        weight_other = jnp.where(later, 1, segments - twin).astype(F32)

        def payload_rows(first, d=d, weight_mine=weight_mine, weight_other=weight_other):
            q = tile_at(core * part + first)
            payload[d - 1, tile_at(first), :] = (
                weight_mine * mine[q, :] + weight_other * other[q, :]
            ).astype(BF16)

        by_rows(part, payload_rows)
        far_copy(d).start()
    for d in range(1, outer):
        far_copy(d).wait_recv()
        far_twin(d, core).start()
    for d in range(1, outer):
        far_twin(d, 1 - core).wait_recv()

    ahead = (segments - sg).astype(F32)
    other_error = core.astype(F32)
    other_back = (segments - sg - 1 + core).astype(F32)
    squares[...] = jnp.zeros_like(squares)
    bias_here = dec_bias[:, span(me, width)]

    def error_rows(first):
        r = tile_at(first)
        here, there = mine[r, :], other[r, :]
        base = bias_here - mlp[r, span(me, width)].astype(F32)
        after = jnp.zeros_like(here)
        for d in range(1, outer):
            before = ((group + outer - d) % outer < group).astype(F32)
            arrived = far[d - 1, r, :].astype(F32)
            base = base + before * arrived
            after = after + (1.0 - before) * arrived
        error = base + other_error * there + here
        squares[...] += error * error
        total = ahead * (base + here) + other_back * there + after
        back[r, span(me, width)] = (total * scale).astype(BF16)

    by_rows(rows, error_rows)

    def back_block(s, k=None):
        r = pl.ds(0, rows) if k is None else pl.ds(k * part, part)
        return back.at[r, span(s, width)]

    def back_tok(s, q):
        return send(
            back_block(s), back_out.at[1, :, span(q, width)], st.at[q], rt.at[q], tok=peer
        )

    def pass_on(s):
        @pl.when(s // per_half == peer)
        def _():
            back_tok(s, s % per_half).start()

    def back_term(s):
        return dot_t(back[:, span(s, width)], dec[:, span(s, width)])

    gather_start(links, 6, back_block, me, square)
    pass_on(me)
    square_sum = jnp.sum(squares[...]) / count
    square_in[0] = jnp.full(square_in.shape[1:], square_sum, F32)
    links.start(10, square_in.at[0], square_in.at[1], shard=x)
    acc[...] = back_term(me)
    gather_pass_x(links, 6, back_block, square)
    pass_on(x)
    gather_pass_y(links, 6, back_block, square)
    pass_on(y)
    links.arrived(10)
    square_in[2] = square_in[0] + square_in[1]
    links.start(11, square_in.at[2], square_in.at[3], shard=y)
    acc[...] += back_term(x) + back_term(y)
    links.arrived(8, 9)
    pass_on(corner)
    acc[...] += back_term(corner)

    def grad_rows(first):
        r = tile_at(first)
        grad_out[0, r, :] = (acc[r, :] * slope[r, :]).astype(BF16)

    by_rows(rows, grad_rows)
    grad_copy = send(grad_out.at[0], grad_out.at[1], sg_.at[0], rg_.at[0], tok=peer)
    grad_copy.start()
    links.arrived(11)
    square_tok[0] = square_in[2] + square_in[3]
    tok_copy = send(square_tok.at[0], square_tok.at[1], sn.at[0], rn.at[0], tok=peer)
    tok_copy.start()

    def own_back(first):
        r = tile_at(first)
        back_out[0, r, :] = back[r, span(tok, half_width)]

    by_rows(rows, own_back)
    tok_copy.wait()
    mse_out[...] = square_tok[0] + square_tok[1]
    code_copy.wait()
    cen_tok().wait_send()
    cen_twin(1 - core).wait_recv()
    cen_twin(core).wait_send()
    for d in range(1, outer):
        far_copy(d).wait_send()
        far_twin(d, core).wait_send()
    links.finish()
    for q in range(per_half):
        back_tok(peer * per_half + q, q).wait()
    grad_copy.wait()


def vmem(count):
    return [pl.BlockSpec(memory_space=pltpu.VMEM)] * count


def sems(*sizes):
    found = []
    for size in sizes:
        found += [pltpu.SemaphoreType.DMA((max(size, 1),))] * 2
    return found


def params(number):
    return pltpu.CompilerParams(
        collective_id=number, has_side_effects=True, vmem_limit_bytes=VMEM_BYTES
    )


def scatter_bufs(lead, rows, width):
    whole, half = lead + (rows, width), lead + (rows // 2, width)
    return [pltpu.VMEM(shape, BF16) for shape in (whole,) * 3 + (half,) * 2 + (whole,) * 2]


def mlp_call(activations, gate_weight, up_weight, down_weight):
    n, outer = lax.axis_size("shard"), lax.axis_size("seg") // 2
    tokens = activations.shape[0]
    chunk, width = gate_weight.shape[1] // n, down_weight.shape[1]
    rows, part, far = tokens // 2, tokens // 4, max(outer - 1, 1)
    return pl.pallas_call(
        functools.partial(mlp_kernel, outer),
        out_shape=jax.ShapeDtypeStruct((tokens, width * n), BF16),
        in_specs=vmem(4),
        out_specs=vmem(1)[0],
        scratch_shapes=[
            *scatter_bufs((2,), rows, 2 * chunk),
            pltpu.VMEM((2, rows, chunk), F32),
            pltpu.VMEM((2, rows, chunk), F32),
            pltpu.VMEM((2, n, rows, chunk), BF16),
            pltpu.VMEM((2, rows, width), F32),
            pltpu.VMEM((2, part, width), F32),
            pltpu.VMEM((2, part, width), BF16),
            pltpu.VMEM((2, far, part, width), BF16),
            *sems(2 * (18 + outer)),
        ],
        compiler_params=params(0),
        name="mlp",
    )(activations, gate_weight, up_weight, down_weight)


def sae_call(mlp, enc, enc_bias, dec, dec_bias, live):
    n, outer = lax.axis_size("shard"), lax.axis_size("seg") // 2
    rows, depth = mlp.shape
    width, latents = depth // n, enc.shape[1]
    part, far, half = rows // 2, max(outer - 1, 1), depth // 2
    tokens = rows * lax.axis_size("tok")
    shape = jax.ShapeDtypeStruct
    return pl.pallas_call(
        functools.partial(sae_kernel, outer, 1.0 / math.sqrt(tokens), tokens * depth),
        out_shape=(
            shape((2, rows, half), BF16),
            shape((2, rows, latents), BF16),
            shape((2, rows, half), BF16),
            shape((2, rows, latents), BF16),
            shape((8, 128), F32),
        ),
        in_specs=vmem(6),
        out_specs=tuple(vmem(5)),
        scratch_shapes=[
            pltpu.VMEM((rows, depth), BF16),
            pltpu.VMEM((rows, latents), F32),
            *scatter_bufs((), rows, width),
            pltpu.VMEM((rows, width), F32),
            pltpu.VMEM((rows, width), F32),
            pltpu.VMEM((far, part, width), BF16),
            pltpu.VMEM((far, rows, width), BF16),
            pltpu.VMEM((rows, depth), BF16),
            pltpu.VMEM((rows, latents), F32),
            pltpu.VMEM((TILE, width), F32),
            pltpu.VMEM((n, 8, 128), F32),
            pltpu.VMEM((2, 8, 128), F32),
            *sems(12, 1, 1, 1, 1, outer - 1, outer - 1, n // 2, 1, 1),
        ],
        compiler_params=params(1),
        name="sae",
    )(mlp, enc, enc_bias, dec, dec_bias, live)


def fits(activations, gate_weight, encoder_weight):
    n, segs, toks = lax.axis_size("shard"), lax.axis_size("seg"), lax.axis_size("tok")
    rows, width = activations.shape
    lanes = (width, gate_weight.shape[1] // n, encoder_weight.shape[1])
    return (
        toks == 2
        and n == 4
        and segs % 2 == 0
        and rows % (4 * TILE) == 0
        and all(size % 128 == 0 for size in lanes)
    )


def local(
    activations,
    gate_weight,
    up_weight,
    down_weight,
    encoder_weight,
    encoder_bias,
    decoder_weight,
    decoder_bias,
    segment_sizes,
):
    if not fits(activations, gate_weight, encoder_weight):
        return plain(
            activations,
            gate_weight,
            up_weight,
            down_weight,
            encoder_weight,
            encoder_bias,
            decoder_weight,
            decoder_bias,
            segment_sizes,
        )
    latents = encoder_weight.shape[1]
    here = jnp.arange(segment_sizes.shape[0]) == lax.axis_index("seg")
    size_here = jnp.sum(jnp.where(here, segment_sizes, 0))
    index = lax.axis_index("shard") * latents + jnp.arange(latents)
    live = (index < size_here).astype(F32)[None, :]
    mlp = mlp_call(activations, gate_weight, up_weight, down_weight)
    cen, codes, back, code_grad, mse = sae_call(
        mlp, encoder_weight, encoder_bias[None, :], decoder_weight, decoder_bias[None, :], live
    )

    def over_tokens(a, b):
        a, b = (value.reshape(-1, value.shape[2]) for value in (a, b))
        return lax.dot_general(a, b, (((0,), (0,)), ((), ())), preferred_element_type=F32)

    return over_tokens(cen, code_grad), over_tokens(codes, back), mse[0, :1]


def solution(mesh):
    in_specs = (
        P("tok", "shard"),
        P("shard", "seg"),
        P("shard", "seg"),
        P("seg", "shard"),
        P(None, ("seg", "shard")),
        P(("seg", "shard")),
        P(("seg", "shard"), None),
        P(),
        P(),
    )
    out_specs = (P("tok", ("seg", "shard")), P(("seg", "shard"), "tok"), P("seg"))
    return jax.shard_map(local, mesh=mesh, in_specs=in_specs, out_specs=out_specs, check_vma=False)
```

```python
import functools
import math

import jax
import jax.numpy as jnp
from jax import lax
from jax.experimental import pallas as pl
from jax.experimental.pallas import tpu as pltpu
from jax.sharding import PartitionSpec as P

MESH = pl.DeviceIdType.MESH
F32 = jnp.float32
BF16 = jnp.bfloat16
TILE = 32
VMEM_BYTES = 52 * 1024 * 1024


def carried_in(value, axis, join, neutral, backward):
    count, mine = (lax.axis_size(axis), lax.axis_index(axis))
    pieces = lax.all_gather(value, axis)
    if backward:
        pieces = pieces[::-1]
        mine = count - 1 - mine
    subtotal = jnp.full_like(value, 0) + jnp.asarray(neutral, value.dtype)

    def hop(position, subtotal):
        longer = join(subtotal, pieces[position])
        return jnp.where(position < mine, longer, subtotal)

    return lax.fori_loop(0, count - 1, hop, subtotal)


def plain(
    activations,
    gate_weight,
    up_weight,
    down_weight,
    encoder_weight,
    encoder_bias,
    decoder_weight,
    decoder_bias,
    segment_sizes,
):
    shard_index = lax.axis_index("shard")
    segment_index = lax.axis_index("seg")
    group_index = lax.axis_index("tok")
    tok_rows = activations.shape[0]
    width_slice = activations.shape[1]
    gate_part = jnp.dot(activations, gate_weight, preferred_element_type=jnp.float32)
    up_part = jnp.dot(activations, up_weight, preferred_element_type=jnp.float32)
    gate_total, up_total = lax.psum((gate_part, up_part), "shard")
    hidden = (jax.nn.gelu(gate_total, approximate=True) * up_total).astype(jnp.bfloat16)
    down_part = jnp.dot(hidden, down_weight, preferred_element_type=jnp.float32)
    mlp_slice = lax.psum(down_part, "seg").astype(jnp.bfloat16)
    mlp_full = lax.all_gather(mlp_slice, "shard", axis=1, tiled=True)
    width = mlp_full.shape[1]
    groups = lax.axis_size("tok")
    tokens_all = tok_rows * groups
    half_width = width // groups
    mlp_float = mlp_full.astype(jnp.float32)
    centered = (mlp_float - decoder_bias).astype(jnp.bfloat16)
    lat_count = encoder_weight.shape[1]
    segment_total = segment_sizes.shape[0]
    size_here = jnp.sum(jnp.where(jnp.arange(segment_total) == segment_index, segment_sizes, 0))
    latent_index = shard_index * lat_count + jnp.arange(lat_count)
    live_mask = latent_index < size_here
    pre_act = jnp.dot(centered, encoder_weight, preferred_element_type=jnp.float32) + encoder_bias
    latent_codes = jnp.where(live_mask, jax.nn.softplus(10.0 * pre_act) / 10.0, 0.0).astype(
        jnp.bfloat16
    )
    slope = jnp.where(live_mask, jax.nn.sigmoid(10.0 * pre_act), 0.0)
    codes_all = lax.all_gather(latent_codes, "tok", axis=0, tiled=True)
    centered_all = lax.all_to_all(centered, "tok", split_axis=1, concat_axis=0, tiled=True)
    columns = decoder_weight
    my_part = lax.psum_scatter(
        lax.dot_general(
            columns, latent_codes, (((0,), (1,)), ((), ())), preferred_element_type=jnp.float32
        ),
        "shard",
        scatter_dimension=0,
        tiled=True,
    )
    column_start = shard_index * width_slice
    target = lax.dynamic_slice_in_dim(mlp_float, column_start, width_slice, 1).T
    bias_slice = lax.dynamic_slice_in_dim(decoder_bias, column_start, width_slice, 0)[:, None]
    blank = jnp.zeros_like(my_part)
    earlier = carried_in(my_part, "seg", jnp.add, blank, False)
    errors = bias_slice + (earlier + my_part) - target
    total_square = lax.psum(jnp.sum(errors * errors), ("shard", "tok"))
    prefix_mse = (total_square / (tokens_all * width)).reshape(1)
    later = carried_in(errors, "seg", jnp.add, blank, True)
    back = ((later + errors) * (1.0 / math.sqrt(tokens_all))).astype(jnp.bfloat16)
    back_all = lax.all_gather(back, "tok", axis=1, tiled=True)
    piece = lax.all_gather(back_all, "shard", axis=0, tiled=True)
    columns = decoder_weight
    own_piece = lax.dynamic_slice_in_dim(piece, group_index * tok_rows, tok_rows, 1)
    code_acc = lax.dot_general(
        own_piece, columns, (((0,), (1,)), ((), ())), preferred_element_type=jnp.float32
    )
    grad_piece = lax.dot_general(
        codes_all, piece, (((0,), (1,)), ((), ())), preferred_element_type=jnp.float32
    )
    code_grad = (code_acc * slope).astype(jnp.bfloat16)
    code_grad_all = lax.all_gather(code_grad, "tok", axis=0, tiled=True)
    grad_encoder = lax.dot_general(
        centered_all, code_grad_all, (((0,), (0,)), ((), ())), preferred_element_type=jnp.float32
    )
    grad_decoder = lax.dynamic_slice_in_dim(grad_piece, group_index * half_width, half_width, 1)
    return (grad_encoder, grad_decoder, prefix_mse)


def send(src, dst, send_sem, recv_sem, **place):
    return pltpu.make_async_remote_copy(
        src_ref=src,
        dst_ref=dst,
        send_sem=send_sem,
        recv_sem=recv_sem,
        device_id=place,
        device_id_type=MESH,
    )


def greet(peers):
    barrier = pltpu.get_barrier_semaphore()
    for place in peers:
        pl.semaphore_signal(barrier, inc=1, device_id=place, device_id_type=MESH)
    pl.semaphore_wait(barrier, len(peers))


def by_rows(total, body):
    def step(i, carry):
        body(i * TILE)
        return carry

    lax.fori_loop(0, total // TILE, step, 0)


def tile_at(first):
    return pl.ds(pl.multiple_of(first, TILE), TILE)


def span(index, size):
    return pl.ds(pl.multiple_of(index * size, 128 if size % 128 == 0 else 32), size)


def dot(a, b):
    return jnp.dot(a, b, preferred_element_type=F32)


def dot_t(a, b):
    return lax.dot_general(a, b, (((1,), (1,)), ((), ())), preferred_element_type=F32)


def gelu_tanh(x):
    return x * (0.5 * (1.0 + jnp.tanh(math.sqrt(2.0 / math.pi) * (x + 0.044715 * (x * x * x)))))


class Links:
    def __init__(self, send_sems, recv_sems):
        self.sems, self.copies = (send_sems, recv_sems), {}

    def start(self, number, src, dst, **place):
        sent, got = (group.at[number] for group in self.sems)
        self.copies[number] = send(src, dst, sent, got, **place)
        self.copies[number].start()

    def arrived(self, *numbers):
        for number in numbers:
            self.copies[number].wait_recv()

    def finish(self):
        for copy in self.copies.values():
            copy.wait_send()


def square_of(me):
    x = me + 1 - 2 * (me % 2)
    y = (me + 2) % 4
    return x, y, (x + 2) % 4


def scatter_start(links, base, fill, square, half, bufs):
    x, y, corner = square
    to_corner, to_x, to_y, via_x, via_y, from_x, from_y = bufs
    top, low = pl.ds(0, half), pl.ds(half, half)
    fill(to_corner, corner)
    links.start(base, to_corner.at[top, :], via_x, shard=x)
    links.start(base + 1, to_corner.at[low, :], via_y, shard=y)
    fill(to_x, x)
    links.start(base + 2, to_x.at[top, :], from_x.at[top, :], shard=x)
    fill(to_y, y)
    links.start(base + 3, to_y.at[low, :], from_y.at[low, :], shard=y)


def scatter_forward(links, base, square, half, bufs):
    x, y, _ = square
    _, to_x, to_y, via_x, via_y, from_x, from_y = bufs
    top, low = pl.ds(0, half), pl.ds(half, half)

    def add_top(first):
        r = tile_at(first)
        to_y[r, :] = (to_y[r, :].astype(F32) + via_x[r, :].astype(F32)).astype(BF16)

    def add_low(first):
        r, q = tile_at(first), tile_at(half + first)
        to_x[q, :] = (to_x[q, :].astype(F32) + via_y[r, :].astype(F32)).astype(BF16)

    links.arrived(base)
    by_rows(half, add_top)
    links.start(base + 4, to_y.at[top, :], from_y.at[top, :], shard=y)
    links.arrived(base + 1)
    by_rows(half, add_low)
    links.start(base + 5, to_x.at[low, :], from_x.at[low, :], shard=x)


def scatter_wait(links, base):
    links.arrived(base + 2, base + 3, base + 4, base + 5)


def gather_start(links, base, block, me, square):
    x, y, _ = square
    links.start(base, block(me), block(me), shard=x)
    links.start(base + 1, block(me), block(me), shard=y)


def gather_pass_x(links, base, block, square):
    x, y, _ = square
    links.arrived(base)
    links.start(base + 2, block(x, 0), block(x, 0), shard=y)


def gather_pass_y(links, base, block, square):
    x, y, _ = square
    links.arrived(base + 1)
    links.start(base + 3, block(y, 1), block(y, 1), shard=x)


def mlp_kernel(
    outer, act, wg, wu, wd, out,
    to_corner, to_x, to_y, via_x, via_y, from_x, from_y,
    gate, up, hid, down, got, half, far, sent, arrived,
):
    me, sg = lax.axis_index("shard"), lax.axis_index("seg")
    core, group = sg % 2, sg // 2
    twin = sg + 1 - 2 * core
    square = square_of(me)
    x, y, corner = square
    chunk = wg.shape[1] // 4
    width = wd.shape[1]
    rows = act.shape[0] // 2
    part = rows // 2
    small = part // 2
    links = Links(sent, arrived)
    stride = 19 + outer - 1
    greet(
        [{"shard": x}, {"shard": y}, {"seg": twin}]
        + [{"seg": ((group + d) % outer) * 2 + core} for d in range(1, outer)]
    )

    def bufs(t):
        return [b.at[t] for b in (to_corner, to_x, to_y, via_x, via_y, from_x, from_y)]

    def tokens(t):
        return act[t * rows : (t + 1) * rows, :]

    def partial_start(t):
        def fill(ref, p):
            ref[:, :chunk] = dot(tokens(t), wg[:, span(p, chunk)]).astype(BF16)
            ref[:, chunk:] = dot(tokens(t), wu[:, span(p, chunk)]).astype(BF16)

        scatter_start(links, t * stride, fill, square, part, bufs(t))

    def partial_forward(t):
        scatter_forward(links, t * stride, square, part, bufs(t))

    def partial_own(t):
        gate[t] = dot(tokens(t), wg[:, span(me, chunk)])
        up[t] = dot(tokens(t), wu[:, span(me, chunk)])

    def hid_block(t):
        def block(s, k=None):
            r = pl.ds(0, rows) if k is None else pl.ds(k * part, part)
            return hid.at[t, s, r, :]

        return block

    def hidden_start(t):
        scatter_wait(links, t * stride)

        def hidden_rows(first):
            r = tile_at(first)
            g = gate[t, r, :] + from_x[t, r, :chunk].astype(F32) + from_y[t, r, :chunk].astype(F32)
            u = up[t, r, :] + from_x[t, r, chunk:].astype(F32) + from_y[t, r, chunk:].astype(F32)
            hid[t, me, r, :] = (gelu_tanh(g) * u).astype(BF16)

        by_rows(rows, hidden_rows)
        gather_start(links, t * stride + 6, hid_block(t), me, square)

    def hidden_forward(t):
        gather_pass_x(links, t * stride + 6, hid_block(t), square)
        gather_pass_y(links, t * stride + 6, hid_block(t), square)

    def term(t, s):
        return dot(hid[t, s], wd[span(s, chunk), :])

    def down_near(t):
        down[t] = term(t, me) + term(t, x) + term(t, y)

    def down_start(t):
        links.arrived(t * stride + 8, t * stride + 9)
        down[t] += term(t, corner)
        links.start(t * stride + 10, down.at[t, span(1 - core, part), :], got.at[t], seg=twin)

    def far_start(t):
        links.arrived(t * stride + 10)

        def half_rows(first):
            r = tile_at(first)
            half[t, r, :] = (down[t, tile_at(core * part + first), :] + got[t, r, :]).astype(BF16)

        by_rows(part, half_rows)
        for d in range(1, outer):
            to = ((group + d) % outer) * 2 + core
            links.start(t * stride + 18 + d, half.at[t], far.at[t, d - 1], seg=to)

    def out_block(t):
        def block(s, k=None):
            first = t * rows + core * part
            if k is None:
                r = pl.ds(pl.multiple_of(first, 32), part)
            else:
                r = pl.ds(pl.multiple_of(first + k * small, 16), small)
            return out.at[r, span(s, width)]

        return block

    def twin_start(t, number, s):
        piece = out_block(t)(s)
        links.start(t * stride + 15 + number, piece, piece, seg=twin)

    def out_start(t):
        for d in range(1, outer):
            links.arrived(t * stride + 18 + d)

        def out_rows(first):
            r = tile_at(first)
            total = half[t, r, :].astype(F32)
            for d in range(outer - 1):
                total = total + far[t, d, r, :].astype(F32)
            out[tile_at(t * rows + core * part + first), span(me, width)] = total.astype(BF16)

        by_rows(part, out_rows)
        gather_start(links, t * stride + 11, out_block(t), me, square)
        twin_start(t, 0, me)

    def out_forward(t):
        gather_pass_x(links, t * stride + 11, out_block(t), square)
        twin_start(t, 1, x)
        gather_pass_y(links, t * stride + 11, out_block(t), square)
        twin_start(t, 2, y)

    def out_last(t):
        links.arrived(t * stride + 13, t * stride + 14)
        twin_start(t, 3, corner)

    partial_start(0)
    partial_forward(0)
    partial_start(1)
    partial_own(0)
    hidden_start(0)
    partial_forward(1)
    partial_own(1)
    hidden_forward(0)
    down_near(0)
    hidden_start(1)
    down_start(0)
    far_start(0)
    hidden_forward(1)
    down_near(1)
    out_start(0)
    down_start(1)
    far_start(1)
    out_forward(0)
    out_last(0)
    out_start(1)
    out_forward(1)
    out_last(1)
    for t in range(2):
        links.arrived(*(t * stride + 15 + k for k in range(4)))
    links.finish()


def sae_kernel(
    outer, scale, count, mlp, enc, enc_bias, dec, dec_bias, live,
    cen_out, code_out, back_out, grad_out, mse_out,
    cen, slope, to_corner, to_x, to_y, via_x, via_y, from_x, from_y, mine, other, payload, far,
    back, acc, squares, square_in, square_tok, sent, arrived, back_sent, back_arrived,
):
    me, sg, tok = lax.axis_index("shard"), lax.axis_index("seg"), lax.axis_index("tok")
    core, group = sg % 2, sg // 2
    twin = sg + 1 - 2 * core
    peer = 1 - tok
    square = square_of(me)
    x, y, corner = square
    links = Links(sent, arrived)
    segments = outer * 2
    tokens, depth = mlp.shape
    width = depth // 4
    half_width = depth // 2
    rows = tokens // 2
    part = rows // 2
    stride = 12 + 2 * (outer - 1)
    code_link, cen_link, cen_twin, near_square, far_square, tok_square = (
        2 * stride + k for k in range(6)
    )
    greet(
        [{"shard": x}, {"shard": y}, {"seg": twin}, {"tok": peer}]
        + [{"seg": ((group + d) % outer) * 2 + core} for d in range(1, outer)]
    )

    def center_rows(first):
        r = tile_at(first)
        cen[r, :] = (mlp[r, :].astype(F32) - dec_bias[...]).astype(BF16)
        cen_out[0, r, :] = cen[r, span(tok, half_width)]

    def bufs(t):
        return [b.at[t] for b in (to_corner, to_x, to_y, via_x, via_y, from_x, from_y)]

    def half_of(t):
        return pl.ds(t * rows, rows)

    latents = enc.shape[1]
    step = 256 if latents % 256 == 0 else 128

    def encode(t):
        def columns(i, carry):
            c = span(i, step)
            pre = 10.0 * (dot(cen[half_of(t), :], enc[:, c]) + enc_bias[:, c])
            on = live[:, c] > 0.0
            soft = jnp.maximum(pre, 0.0) + jnp.log1p(jnp.exp(-jnp.abs(pre)))
            code_out[0, half_of(t), c] = jnp.where(on, soft / 10.0, 0.0).astype(BF16)
            slope[half_of(t), c] = jnp.where(on, jax.nn.sigmoid(pre), 0.0)
            return carry

        lax.fori_loop(0, latents // step, columns, 0)

    def part_start(t):
        def fill(ref, p):
            ref[...] = dot(code_out[0, half_of(t), :], dec[:, span(p, width)]).astype(BF16)

        scatter_start(links, t * stride, fill, square, part, bufs(t))

    def part_forward(t):
        scatter_forward(links, t * stride, square, part, bufs(t))

    def part_own(t):
        mine[half_of(t), :] = dot(code_out[0, half_of(t), :], dec[:, span(me, width)])

    def part_sum(t):
        scatter_wait(links, t * stride)

        def mine_rows(first):
            r, q = tile_at(first), tile_at(t * rows + first)
            mine[q, :] = mine[q, :] + from_x[t, r, :].astype(F32) + from_y[t, r, :].astype(F32)

        by_rows(rows, mine_rows)
        links.start(
            t * stride + 10, mine.at[half_of(t), :], other.at[half_of(t), :], seg=twin
        )

    def core_rows(t):
        return pl.ds(pl.multiple_of(t * rows + core * part, TILE), part)

    def far_start(t):
        links.arrived(t * stride + 10)
        for d in range(1, outer):
            to = (group + d) % outer
            later = to > group
            weight_mine = jnp.where(later, 1, segments - sg).astype(F32)
            weight_other = jnp.where(later, 1, segments - twin).astype(F32)

            def payload_rows(first, d=d, weight_mine=weight_mine, weight_other=weight_other):
                q = tile_at(t * rows + core * part + first)
                payload[t, d - 1, tile_at(first), :] = (
                    weight_mine * mine[q, :] + weight_other * other[q, :]
                ).astype(BF16)

            by_rows(part, payload_rows)
            links.start(
                t * stride + 11 + d,
                payload.at[t, d - 1],
                far.at[d - 1, core_rows(t), :],
                seg=to * 2 + core,
            )

    def far_pass(t):
        for d in range(1, outer):
            links.arrived(t * stride + 11 + d)
            piece = far.at[d - 1, core_rows(t), :]
            links.start(t * stride + 10 + outer + d, piece, piece, seg=twin)

    ahead = (segments - sg).astype(F32)
    other_error = core.astype(F32)
    other_back = (segments - sg - 1 + core).astype(F32)
    bias_here = dec_bias[:, span(me, width)]

    def back_block(t):
        def block(s, k=None):
            r = half_of(t) if k is None else pl.ds(t * rows + k * part, part)
            return back.at[r, span(s, width)]

        return block

    def back_tok(t, s):
        q = s % 2
        return send(
            back_block(t)(s),
            back_out.at[1, half_of(t), span(q, width)],
            back_sent.at[t * 2 + q],
            back_arrived.at[t * 2 + q],
            tok=peer,
        )

    def pass_on(t, s):
        @pl.when(s // 2 == peer)
        def _():
            back_tok(t, s).start()

    def back_start(t):
        for d in range(1, outer):
            links.arrived(t * stride + 10 + outer + d)

        def error_rows(first):
            r = tile_at(t * rows + first)
            here, there = mine[r, :], other[r, :]
            base = bias_here - mlp[r, span(me, width)].astype(F32)
            after = jnp.zeros_like(here)
            for d in range(1, outer):
                before = ((group + outer - d) % outer < group).astype(F32)
                came = far[d - 1, r, :].astype(F32)
                base = base + before * came
                after = after + (1.0 - before) * came
            error = base + other_error * there + here
            squares[...] += error * error
            total = ahead * (base + here) + other_back * there + after
            back[r, span(me, width)] = (total * scale).astype(BF16)

        by_rows(rows, error_rows)
        gather_start(links, t * stride + 6, back_block(t), me, square)
        pass_on(t, me)

    def back_term(t, s):
        return dot_t(back[half_of(t), span(s, width)], dec[:, span(s, width)])

    def back_forward(t):
        gather_pass_x(links, t * stride + 6, back_block(t), square)
        pass_on(t, x)
        gather_pass_y(links, t * stride + 6, back_block(t), square)
        pass_on(t, y)

    def back_near(t):
        acc[half_of(t), :] = back_term(t, me) + back_term(t, x) + back_term(t, y)

    def back_last(t):
        links.arrived(t * stride + 8, t * stride + 9)
        pass_on(t, corner)
        acc[half_of(t), :] += back_term(t, corner)

        def grad_rows(first):
            r = tile_at(t * rows + first)
            grad_out[0, r, :] = (acc[r, :] * slope[r, :]).astype(BF16)

        by_rows(rows, grad_rows)
        links.start(
            t * stride + 11,
            grad_out.at[0, half_of(t), :],
            grad_out.at[1, half_of(t), :],
            tok=peer,
        )

    squares[...] = jnp.zeros_like(squares)
    by_rows(tokens, center_rows)
    encode(0)
    part_start(0)
    links.start(
        cen_link,
        cen.at[span(core, rows), span(peer, half_width)],
        cen_out.at[1, span(core, rows), :],
        tok=peer,
    )
    encode(1)
    part_forward(0)
    part_start(1)
    part_own(0)
    part_sum(0)
    part_forward(1)
    far_start(0)
    part_own(1)
    links.start(code_link, code_out.at[0], code_out.at[1], tok=peer)
    far_pass(0)
    part_sum(1)
    back_start(0)
    far_start(1)
    back_forward(0)
    far_pass(1)
    back_near(0)
    back_start(1)
    back_last(0)
    square_sum = jnp.sum(squares[...]) / count
    square_in[0] = jnp.full(square_in.shape[1:], square_sum, F32)
    links.start(near_square, square_in.at[0], square_in.at[1], shard=x)
    back_forward(1)
    back_near(1)
    links.arrived(near_square)
    square_in[2] = square_in[0] + square_in[1]
    links.start(far_square, square_in.at[2], square_in.at[3], shard=y)
    back_last(1)
    links.arrived(far_square)
    square_tok[0] = square_in[2] + square_in[3]
    links.start(tok_square, square_tok.at[0], square_tok.at[1], tok=peer)
    links.arrived(cen_link)
    piece = cen_out.at[1, span(core, rows), :]
    links.start(cen_twin, piece, piece, seg=twin)

    def own_back(first):
        r = tile_at(first)
        back_out[0, r, :] = back[r, span(tok, half_width)]

    by_rows(tokens, own_back)
    links.arrived(tok_square)
    mse_out[...] = square_tok[0] + square_tok[1]
    links.arrived(code_link, cen_twin)
    for t in range(2):
        for q in range(2):
            back_tok(t, peer * 2 + q).wait()
        links.arrived(t * stride + 11)
    links.finish()


def vmem(count):
    return [pl.BlockSpec(memory_space=pltpu.VMEM)] * count


def sems(*sizes):
    found = []
    for size in sizes:
        found += [pltpu.SemaphoreType.DMA((max(size, 1),))] * 2
    return found


def params(number):
    return pltpu.CompilerParams(
        collective_id=number, has_side_effects=True, vmem_limit_bytes=VMEM_BYTES
    )


def scatter_bufs(lead, rows, width):
    whole, half = lead + (rows, width), lead + (rows // 2, width)
    return [pltpu.VMEM(shape, BF16) for shape in (whole,) * 3 + (half,) * 2 + (whole,) * 2]


def mlp_call(activations, gate_weight, up_weight, down_weight):
    n, outer = lax.axis_size("shard"), lax.axis_size("seg") // 2
    tokens = activations.shape[0]
    chunk, width = gate_weight.shape[1] // n, down_weight.shape[1]
    rows, part, far = tokens // 2, tokens // 4, max(outer - 1, 1)
    return pl.pallas_call(
        functools.partial(mlp_kernel, outer),
        out_shape=jax.ShapeDtypeStruct((tokens, width * n), BF16),
        in_specs=vmem(4),
        out_specs=vmem(1)[0],
        scratch_shapes=[
            *scatter_bufs((2,), rows, 2 * chunk),
            pltpu.VMEM((2, rows, chunk), F32),
            pltpu.VMEM((2, rows, chunk), F32),
            pltpu.VMEM((2, n, rows, chunk), BF16),
            pltpu.VMEM((2, rows, width), F32),
            pltpu.VMEM((2, part, width), F32),
            pltpu.VMEM((2, part, width), BF16),
            pltpu.VMEM((2, far, part, width), BF16),
            *sems(2 * (18 + outer)),
        ],
        compiler_params=params(0),
        name="mlp",
    )(activations, gate_weight, up_weight, down_weight)


def sae_call(mlp, enc, enc_bias, dec, dec_bias, live):
    n, outer = lax.axis_size("shard"), lax.axis_size("seg") // 2
    rows, depth = mlp.shape
    width, latents = depth // n, enc.shape[1]
    part, far, half = rows // 4, max(outer - 1, 1), depth // 2
    tokens = rows * lax.axis_size("tok")
    shape = jax.ShapeDtypeStruct
    return pl.pallas_call(
        functools.partial(sae_kernel, outer, 1.0 / math.sqrt(tokens), tokens * depth),
        out_shape=(
            shape((2, rows, half), BF16),
            shape((2, rows, latents), BF16),
            shape((2, rows, half), BF16),
            shape((2, rows, latents), BF16),
            shape((8, 128), F32),
        ),
        in_specs=vmem(6),
        out_specs=tuple(vmem(5)),
        scratch_shapes=[
            pltpu.VMEM((rows, depth), BF16),
            pltpu.VMEM((rows, latents), F32),
            *scatter_bufs((2,), rows // 2, width),
            pltpu.VMEM((rows, width), F32),
            pltpu.VMEM((rows, width), F32),
            pltpu.VMEM((2, far, part, width), BF16),
            pltpu.VMEM((far, rows, width), BF16),
            pltpu.VMEM((rows, depth), BF16),
            pltpu.VMEM((rows, latents), F32),
            pltpu.VMEM((TILE, width), F32),
            pltpu.VMEM((n, 8, 128), F32),
            pltpu.VMEM((2, 8, 128), F32),
            *sems(30 + 4 * (outer - 1), 4),
        ],
        compiler_params=params(1),
        name="sae",
    )(mlp, enc, enc_bias, dec, dec_bias, live)


def fits(activations, gate_weight, encoder_weight):
    n, segs, toks = lax.axis_size("shard"), lax.axis_size("seg"), lax.axis_size("tok")
    rows, width = activations.shape
    lanes = (width, gate_weight.shape[1] // n, encoder_weight.shape[1])
    return (
        toks == 2
        and n == 4
        and segs % 2 == 0
        and rows % (4 * TILE) == 0
        and all(size % 128 == 0 for size in lanes)
    )


def local(
    activations,
    gate_weight,
    up_weight,
    down_weight,
    encoder_weight,
    encoder_bias,
    decoder_weight,
    decoder_bias,
    segment_sizes,
):
    if not fits(activations, gate_weight, encoder_weight):
        return plain(
            activations,
            gate_weight,
            up_weight,
            down_weight,
            encoder_weight,
            encoder_bias,
            decoder_weight,
            decoder_bias,
            segment_sizes,
        )
    latents = encoder_weight.shape[1]
    here = jnp.arange(segment_sizes.shape[0]) == lax.axis_index("seg")
    size_here = jnp.sum(jnp.where(here, segment_sizes, 0))
    index = lax.axis_index("shard") * latents + jnp.arange(latents)
    live = (index < size_here).astype(F32)[None, :]
    mlp = mlp_call(activations, gate_weight, up_weight, down_weight)
    cen, codes, back, code_grad, mse = sae_call(
        mlp, encoder_weight, encoder_bias[None, :], decoder_weight, decoder_bias[None, :], live
    )

    def over_tokens(a, b):
        a, b = (value.reshape(-1, value.shape[2]) for value in (a, b))
        return lax.dot_general(a, b, (((0,), (0,)), ((), ())), preferred_element_type=F32)

    return over_tokens(cen, code_grad), over_tokens(codes, back), mse[0, :1]


def solution(mesh):
    in_specs = (
        P("tok", "shard"),
        P("shard", "seg"),
        P("shard", "seg"),
        P("seg", "shard"),
        P(None, ("seg", "shard")),
        P(("seg", "shard")),
        P(("seg", "shard"), None),
        P(),
        P(),
    )
    out_specs = (P("tok", ("seg", "shard")), P(("seg", "shard"), "tok"), P("seg"))
    return jax.shard_map(local, mesh=mesh, in_specs=in_specs, out_specs=out_specs, check_vma=False)
```

```python
import functools
import math

import jax
import jax.numpy as jnp
from jax import lax
from jax.experimental import pallas as pl
from jax.experimental.pallas import tpu as pltpu
from jax.sharding import PartitionSpec as P

MESH = pl.DeviceIdType.MESH
F32 = jnp.float32
BF16 = jnp.bfloat16
TILE = 32
VMEM_BYTES = 52 * 1024 * 1024


def carried_in(value, axis, join, neutral, backward):
    count, mine = (lax.axis_size(axis), lax.axis_index(axis))
    pieces = lax.all_gather(value, axis)
    if backward:
        pieces = pieces[::-1]
        mine = count - 1 - mine
    subtotal = jnp.full_like(value, 0) + jnp.asarray(neutral, value.dtype)

    def hop(position, subtotal):
        longer = join(subtotal, pieces[position])
        return jnp.where(position < mine, longer, subtotal)

    return lax.fori_loop(0, count - 1, hop, subtotal)


def plain(
    activations,
    gate_weight,
    up_weight,
    down_weight,
    encoder_weight,
    encoder_bias,
    decoder_weight,
    decoder_bias,
    segment_sizes,
):
    shard_index = lax.axis_index("shard")
    segment_index = lax.axis_index("seg")
    group_index = lax.axis_index("tok")
    tok_rows = activations.shape[0]
    width_slice = activations.shape[1]
    gate_part = jnp.dot(activations, gate_weight, preferred_element_type=jnp.float32)
    up_part = jnp.dot(activations, up_weight, preferred_element_type=jnp.float32)
    gate_total, up_total = lax.psum((gate_part, up_part), "shard")
    hidden = (jax.nn.gelu(gate_total, approximate=True) * up_total).astype(jnp.bfloat16)
    down_part = jnp.dot(hidden, down_weight, preferred_element_type=jnp.float32)
    mlp_slice = lax.psum(down_part, "seg").astype(jnp.bfloat16)
    mlp_full = lax.all_gather(mlp_slice, "shard", axis=1, tiled=True)
    width = mlp_full.shape[1]
    groups = lax.axis_size("tok")
    tokens_all = tok_rows * groups
    half_width = width // groups
    mlp_float = mlp_full.astype(jnp.float32)
    centered = (mlp_float - decoder_bias).astype(jnp.bfloat16)
    lat_count = encoder_weight.shape[1]
    segment_total = segment_sizes.shape[0]
    size_here = jnp.sum(jnp.where(jnp.arange(segment_total) == segment_index, segment_sizes, 0))
    latent_index = shard_index * lat_count + jnp.arange(lat_count)
    live_mask = latent_index < size_here
    pre_act = jnp.dot(centered, encoder_weight, preferred_element_type=jnp.float32) + encoder_bias
    latent_codes = jnp.where(live_mask, jax.nn.softplus(10.0 * pre_act) / 10.0, 0.0).astype(
        jnp.bfloat16
    )
    slope = jnp.where(live_mask, jax.nn.sigmoid(10.0 * pre_act), 0.0)
    codes_all = lax.all_gather(latent_codes, "tok", axis=0, tiled=True)
    centered_all = lax.all_to_all(centered, "tok", split_axis=1, concat_axis=0, tiled=True)
    columns = decoder_weight
    my_part = lax.psum_scatter(
        lax.dot_general(
            columns, latent_codes, (((0,), (1,)), ((), ())), preferred_element_type=jnp.float32
        ),
        "shard",
        scatter_dimension=0,
        tiled=True,
    )
    column_start = shard_index * width_slice
    target = lax.dynamic_slice_in_dim(mlp_float, column_start, width_slice, 1).T
    bias_slice = lax.dynamic_slice_in_dim(decoder_bias, column_start, width_slice, 0)[:, None]
    blank = jnp.zeros_like(my_part)
    earlier = carried_in(my_part, "seg", jnp.add, blank, False)
    errors = bias_slice + (earlier + my_part) - target
    total_square = lax.psum(jnp.sum(errors * errors), ("shard", "tok"))
    prefix_mse = (total_square / (tokens_all * width)).reshape(1)
    later = carried_in(errors, "seg", jnp.add, blank, True)
    back = ((later + errors) * (1.0 / math.sqrt(tokens_all))).astype(jnp.bfloat16)
    back_all = lax.all_gather(back, "tok", axis=1, tiled=True)
    piece = lax.all_gather(back_all, "shard", axis=0, tiled=True)
    columns = decoder_weight
    own_piece = lax.dynamic_slice_in_dim(piece, group_index * tok_rows, tok_rows, 1)
    code_acc = lax.dot_general(
        own_piece, columns, (((0,), (1,)), ((), ())), preferred_element_type=jnp.float32
    )
    grad_piece = lax.dot_general(
        codes_all, piece, (((0,), (1,)), ((), ())), preferred_element_type=jnp.float32
    )
    code_grad = (code_acc * slope).astype(jnp.bfloat16)
    code_grad_all = lax.all_gather(code_grad, "tok", axis=0, tiled=True)
    grad_encoder = lax.dot_general(
        centered_all, code_grad_all, (((0,), (0,)), ((), ())), preferred_element_type=jnp.float32
    )
    grad_decoder = lax.dynamic_slice_in_dim(grad_piece, group_index * half_width, half_width, 1)
    return (grad_encoder, grad_decoder, prefix_mse)


def send(src, dst, send_sem, recv_sem, **place):
    return pltpu.make_async_remote_copy(
        src_ref=src,
        dst_ref=dst,
        send_sem=send_sem,
        recv_sem=recv_sem,
        device_id=place,
        device_id_type=MESH,
    )


def greet(peers):
    barrier = pltpu.get_barrier_semaphore()
    for place in peers:
        pl.semaphore_signal(barrier, inc=1, device_id=place, device_id_type=MESH)
    pl.semaphore_wait(barrier, len(peers))


def by_rows(total, body):
    def step(i, carry):
        body(i * TILE)
        return carry

    lax.fori_loop(0, total // TILE, step, 0)


def tile_at(first):
    return pl.ds(pl.multiple_of(first, TILE), TILE)


def span(index, size):
    return pl.ds(pl.multiple_of(index * size, 128 if size % 128 == 0 else 32), size)


def dot(a, b):
    return jnp.dot(a, b, preferred_element_type=F32)


def dot_t(a, b):
    return lax.dot_general(a, b, (((1,), (1,)), ((), ())), preferred_element_type=F32)


def gelu_tanh(x):
    return x * (0.5 * (1.0 + jnp.tanh(math.sqrt(2.0 / math.pi) * (x + 0.044715 * (x * x * x)))))


class Links:
    def __init__(self, send_sems, recv_sems):
        self.sems, self.copies = (send_sems, recv_sems), {}

    def start(self, number, src, dst, **place):
        sent, got = (group.at[number] for group in self.sems)
        self.copies[number] = send(src, dst, sent, got, **place)
        self.copies[number].start()

    def arrived(self, *numbers):
        for number in numbers:
            self.copies[number].wait_recv()

    def finish(self):
        for copy in self.copies.values():
            copy.wait_send()


def square_of(me):
    x = me + 1 - 2 * (me % 2)
    y = (me + 2) % 4
    return x, y, (x + 2) % 4


def scatter_start(links, base, fill, square, half, bufs):
    x, y, corner = square
    to_corner, to_x, to_y, via_x, via_y, from_x, from_y = bufs
    top, low = pl.ds(0, half), pl.ds(half, half)
    fill(to_corner, corner)
    links.start(base, to_corner.at[top, :], via_x, shard=x)
    links.start(base + 1, to_corner.at[low, :], via_y, shard=y)
    fill(to_x, x)
    links.start(base + 2, to_x.at[top, :], from_x.at[top, :], shard=x)
    fill(to_y, y)
    links.start(base + 3, to_y.at[low, :], from_y.at[low, :], shard=y)


def scatter_forward(links, base, square, half, bufs):
    x, y, _ = square
    _, to_x, to_y, via_x, via_y, from_x, from_y = bufs
    top, low = pl.ds(0, half), pl.ds(half, half)

    def add_top(first):
        r = tile_at(first)
        to_y[r, :] = (to_y[r, :].astype(F32) + via_x[r, :].astype(F32)).astype(BF16)

    def add_low(first):
        r, q = tile_at(first), tile_at(half + first)
        to_x[q, :] = (to_x[q, :].astype(F32) + via_y[r, :].astype(F32)).astype(BF16)

    links.arrived(base)
    by_rows(half, add_top)
    links.start(base + 4, to_y.at[top, :], from_y.at[top, :], shard=y)
    links.arrived(base + 1)
    by_rows(half, add_low)
    links.start(base + 5, to_x.at[low, :], from_x.at[low, :], shard=x)


def scatter_wait(links, base):
    links.arrived(base + 2, base + 3, base + 4, base + 5)


def gather_start(links, base, block, me, square):
    x, y, _ = square
    links.start(base, block(me), block(me), shard=x)
    links.start(base + 1, block(me), block(me), shard=y)


def gather_pass_x(links, base, block, square):
    x, y, _ = square
    links.arrived(base)
    links.start(base + 2, block(x, 0), block(x, 0), shard=y)


def gather_pass_y(links, base, block, square):
    x, y, _ = square
    links.arrived(base + 1)
    links.start(base + 3, block(y, 1), block(y, 1), shard=x)


def mlp_steps(
    outer, down_ready, act, wg, wu, wd, out,
    to_corner, to_x, to_y, via_x, via_y, from_x, from_y,
    gate, up, hid, down, got, half, far, sent, arrived,
):
    me, sg = lax.axis_index("shard"), lax.axis_index("seg")
    core, group = sg % 2, sg // 2
    twin = sg + 1 - 2 * core
    square = square_of(me)
    x, y, corner = square
    chunk = wg.shape[1] // 4
    width = wd.shape[1]
    rows = act.shape[0] // 2
    part = rows // 2
    small = part // 2
    links = Links(sent, arrived)
    stride = 19 + outer - 1
    def bufs(t):
        return [b.at[t] for b in (to_corner, to_x, to_y, via_x, via_y, from_x, from_y)]

    def tokens(t):
        return act[t * rows : (t + 1) * rows, :]

    def partial_start(t):
        def fill(ref, p):
            ref[:, :chunk] = dot(tokens(t), wg[:, span(p, chunk)]).astype(BF16)
            ref[:, chunk:] = dot(tokens(t), wu[:, span(p, chunk)]).astype(BF16)

        scatter_start(links, t * stride, fill, square, part, bufs(t))

    def partial_forward(t):
        scatter_forward(links, t * stride, square, part, bufs(t))

    def partial_own(t):
        gate[t] = dot(tokens(t), wg[:, span(me, chunk)])
        up[t] = dot(tokens(t), wu[:, span(me, chunk)])

    def hid_block(t):
        def block(s, k=None):
            r = pl.ds(0, rows) if k is None else pl.ds(k * part, part)
            return hid.at[t, s, r, :]

        return block

    def hidden_start(t):
        scatter_wait(links, t * stride)

        def hidden_rows(first):
            r = tile_at(first)
            g = gate[t, r, :] + from_x[t, r, :chunk].astype(F32) + from_y[t, r, :chunk].astype(F32)
            u = up[t, r, :] + from_x[t, r, chunk:].astype(F32) + from_y[t, r, chunk:].astype(F32)
            hid[t, me, r, :] = (gelu_tanh(g) * u).astype(BF16)

        by_rows(rows, hidden_rows)
        gather_start(links, t * stride + 6, hid_block(t), me, square)

    def hidden_forward(t):
        gather_pass_x(links, t * stride + 6, hid_block(t), square)
        gather_pass_y(links, t * stride + 6, hid_block(t), square)

    def term(t, s):
        return dot(hid[t, s], wd[span(s, chunk), :])

    def down_near(t):
        down[t] = term(t, me) + term(t, x) + term(t, y)

    def down_start(t):
        links.arrived(t * stride + 8, t * stride + 9)
        down[t] += term(t, corner)
        links.start(t * stride + 10, down.at[t, span(1 - core, part), :], got.at[t], seg=twin)

    def far_start(t):
        links.arrived(t * stride + 10)

        def half_rows(first):
            r = tile_at(first)
            half[t, r, :] = (down[t, tile_at(core * part + first), :] + got[t, r, :]).astype(BF16)

        by_rows(part, half_rows)
        for d in range(1, outer):
            to = ((group + d) % outer) * 2 + core
            links.start(t * stride + 18 + d, half.at[t], far.at[t, d - 1], seg=to)

    def out_block(t):
        def block(s, k=None):
            first = t * rows + core * part
            if k is None:
                r = pl.ds(pl.multiple_of(first, 32), part)
            else:
                r = pl.ds(pl.multiple_of(first + k * small, 16), small)
            return out.at[r, span(s, width)]

        return block

    def twin_start(t, number, s):
        piece = out_block(t)(s)
        links.start(t * stride + 15 + number, piece, piece, seg=twin)

    def out_start(t):
        for d in range(1, outer):
            links.arrived(t * stride + 18 + d)

        def out_rows(first):
            r = tile_at(first)
            total = half[t, r, :].astype(F32)
            for d in range(outer - 1):
                total = total + far[t, d, r, :].astype(F32)
            out[tile_at(t * rows + core * part + first), span(me, width)] = total.astype(BF16)

        by_rows(part, out_rows)
        gather_start(links, t * stride + 11, out_block(t), me, square)
        twin_start(t, 0, me)

    def out_forward(t):
        gather_pass_x(links, t * stride + 11, out_block(t), square)
        twin_start(t, 1, x)
        gather_pass_y(links, t * stride + 11, out_block(t), square)
        twin_start(t, 2, y)

    def out_last(t):
        links.arrived(t * stride + 13, t * stride + 14)
        twin_start(t, 3, corner)

    partial_start(0)
    partial_forward(0)
    partial_start(1)
    partial_own(0)
    hidden_start(0)
    partial_forward(1)
    partial_own(1)
    hidden_forward(0)
    down_ready()
    down_near(0)
    hidden_start(1)
    down_start(0)
    far_start(0)
    hidden_forward(1)
    down_near(1)
    out_start(0)
    down_start(1)
    far_start(1)
    out_forward(0)
    out_last(0)
    out_start(1)
    links.arrived(*(15 + k for k in range(4)))
    yield
    out_forward(1)
    yield
    out_last(1)
    links.arrived(*(stride + 15 + k for k in range(4)))
    yield
    links.finish()
    yield


def sae_steps(
    outer, scale, count, mlp, enc, enc_bias, dec, dec_bias, sizes,
    cen_out, code_out, back_out, grad_out, mse_out,
    cen, slope, to_corner, to_x, to_y, via_x, via_y, from_x, from_y, mine, other, payload, far,
    back, acc, squares, square_in, square_tok, sent, arrived, back_sent, back_arrived,
):
    me, sg, tok = lax.axis_index("shard"), lax.axis_index("seg"), lax.axis_index("tok")
    core, group = sg % 2, sg // 2
    twin = sg + 1 - 2 * core
    peer = 1 - tok
    square = square_of(me)
    x, y, corner = square
    links = Links(sent, arrived)
    segments = outer * 2
    tokens, depth = mlp.shape
    width = depth // 4
    half_width = depth // 2
    rows = tokens // 2
    part = rows // 2
    stride = 12 + 2 * (outer - 1)
    code_link, cen_link, cen_twin, near_square, far_square, tok_square = (
        2 * stride + k for k in range(6)
    )
    def center_rows(first):
        r = tile_at(first)
        cen[r, :] = (mlp[r, :].astype(F32) - dec_bias[...]).astype(BF16)
        cen_out[0, r, :] = cen[r, span(tok, half_width)]

    def bufs(t):
        return [b.at[t] for b in (to_corner, to_x, to_y, via_x, via_y, from_x, from_y)]

    def half_of(t):
        return pl.ds(t * rows, rows)

    latents = enc.shape[1]
    step = 256 if latents % 256 == 0 else 128

    def encode(t):
        def columns(i, carry):
            c = span(i, step)
            pre = 10.0 * (dot(cen[half_of(t), :], enc[:, c]) + enc_bias[:, c])
            index = me * latents + i * step + lax.broadcasted_iota(jnp.int32, (1, step), 1)
            on = index < sizes[sg]
            soft = jnp.maximum(pre, 0.0) + jnp.log1p(jnp.exp(-jnp.abs(pre)))
            code_out[0, half_of(t), c] = jnp.where(on, soft / 10.0, 0.0).astype(BF16)
            slope[half_of(t), c] = jnp.where(on, jax.nn.sigmoid(pre), 0.0)
            return carry

        lax.fori_loop(0, latents // step, columns, 0)

    def part_start(t):
        def fill(ref, p):
            ref[...] = dot(code_out[0, half_of(t), :], dec[:, span(p, width)]).astype(BF16)

        scatter_start(links, t * stride, fill, square, part, bufs(t))

    def part_forward(t):
        scatter_forward(links, t * stride, square, part, bufs(t))

    def part_own(t):
        mine[half_of(t), :] = dot(code_out[0, half_of(t), :], dec[:, span(me, width)])

    def part_sum(t):
        scatter_wait(links, t * stride)

        def mine_rows(first):
            r, q = tile_at(first), tile_at(t * rows + first)
            mine[q, :] = mine[q, :] + from_x[t, r, :].astype(F32) + from_y[t, r, :].astype(F32)

        by_rows(rows, mine_rows)
        links.start(
            t * stride + 10, mine.at[half_of(t), :], other.at[half_of(t), :], seg=twin
        )

    def core_rows(t):
        return pl.ds(pl.multiple_of(t * rows + core * part, TILE), part)

    def far_start(t):
        links.arrived(t * stride + 10)
        for d in range(1, outer):
            to = (group + d) % outer
            later = to > group
            weight_mine = jnp.where(later, 1, segments - sg).astype(F32)
            weight_other = jnp.where(later, 1, segments - twin).astype(F32)

            def payload_rows(first, d=d, weight_mine=weight_mine, weight_other=weight_other):
                q = tile_at(t * rows + core * part + first)
                payload[t, d - 1, tile_at(first), :] = (
                    weight_mine * mine[q, :] + weight_other * other[q, :]
                ).astype(BF16)

            by_rows(part, payload_rows)
            links.start(
                t * stride + 11 + d,
                payload.at[t, d - 1],
                far.at[d - 1, core_rows(t), :],
                seg=to * 2 + core,
            )

    def far_pass(t):
        for d in range(1, outer):
            links.arrived(t * stride + 11 + d)
            piece = far.at[d - 1, core_rows(t), :]
            links.start(t * stride + 10 + outer + d, piece, piece, seg=twin)

    ahead = (segments - sg).astype(F32)
    other_error = core.astype(F32)
    other_back = (segments - sg - 1 + core).astype(F32)
    bias_here = dec_bias[:, span(me, width)]

    def back_block(t):
        def block(s, k=None):
            r = half_of(t) if k is None else pl.ds(t * rows + k * part, part)
            return back.at[r, span(s, width)]

        return block

    def back_tok(t, s):
        q = s % 2
        return send(
            back_block(t)(s),
            back_out.at[1, half_of(t), span(q, width)],
            back_sent.at[t * 2 + q],
            back_arrived.at[t * 2 + q],
            tok=peer,
        )

    def pass_on(t, s):
        @pl.when(s // 2 == peer)
        def _():
            back_tok(t, s).start()

    def back_start(t):
        for d in range(1, outer):
            links.arrived(t * stride + 10 + outer + d)

        def error_rows(first):
            r = tile_at(t * rows + first)
            here, there = mine[r, :], other[r, :]
            base = bias_here - mlp[r, span(me, width)].astype(F32)
            after = jnp.zeros_like(here)
            for d in range(1, outer):
                before = ((group + outer - d) % outer < group).astype(F32)
                came = far[d - 1, r, :].astype(F32)
                base = base + before * came
                after = after + (1.0 - before) * came
            error = base + other_error * there + here
            squares[...] += error * error
            total = ahead * (base + here) + other_back * there + after
            back[r, span(me, width)] = (total * scale).astype(BF16)

        by_rows(rows, error_rows)
        gather_start(links, t * stride + 6, back_block(t), me, square)
        pass_on(t, me)

    def back_term(t, s):
        return dot_t(back[half_of(t), span(s, width)], dec[:, span(s, width)])

    def back_forward(t):
        gather_pass_x(links, t * stride + 6, back_block(t), square)
        pass_on(t, x)
        gather_pass_y(links, t * stride + 6, back_block(t), square)
        pass_on(t, y)

    def back_near(t):
        acc[half_of(t), :] = back_term(t, me) + back_term(t, x) + back_term(t, y)

    def back_last(t):
        links.arrived(t * stride + 8, t * stride + 9)
        pass_on(t, corner)
        acc[half_of(t), :] += back_term(t, corner)

        def grad_rows(first):
            r = tile_at(t * rows + first)
            grad_out[0, r, :] = (acc[r, :] * slope[r, :]).astype(BF16)

        by_rows(rows, grad_rows)
        links.start(
            t * stride + 11,
            grad_out.at[0, half_of(t), :],
            grad_out.at[1, half_of(t), :],
            tok=peer,
        )

    squares[...] = jnp.zeros_like(squares)
    by_rows(rows, center_rows)
    encode(0)
    yield
    part_start(0)
    yield
    by_rows(rows, lambda first: center_rows(rows + first))
    links.start(
        cen_link,
        cen.at[span(core, rows), span(peer, half_width)],
        cen_out.at[1, span(core, rows), :],
        tok=peer,
    )
    encode(1)
    part_forward(0)
    part_start(1)
    part_own(0)
    part_sum(0)
    part_forward(1)
    far_start(0)
    part_own(1)
    links.start(code_link, code_out.at[0], code_out.at[1], tok=peer)
    far_pass(0)
    part_sum(1)
    back_start(0)
    far_start(1)
    back_forward(0)
    far_pass(1)
    back_near(0)
    back_start(1)
    back_last(0)
    square_sum = jnp.sum(squares[...]) / count
    square_in[0] = jnp.full(square_in.shape[1:], square_sum, F32)
    links.start(near_square, square_in.at[0], square_in.at[1], shard=x)
    back_forward(1)
    back_near(1)
    links.arrived(near_square)
    square_in[2] = square_in[0] + square_in[1]
    links.start(far_square, square_in.at[2], square_in.at[3], shard=y)
    back_last(1)
    links.arrived(far_square)
    square_tok[0] = square_in[2] + square_in[3]
    links.start(tok_square, square_tok.at[0], square_tok.at[1], tok=peer)
    links.arrived(cen_link)
    piece = cen_out.at[1, span(core, rows), :]
    links.start(cen_twin, piece, piece, seg=twin)

    def own_back(first):
        r = tile_at(first)
        back_out[0, r, :] = back[r, span(tok, half_width)]

    by_rows(tokens, own_back)
    links.arrived(tok_square)
    mse_out[...] = square_tok[0] + square_tok[1]
    links.arrived(code_link, cen_twin)
    for t in range(2):
        for q in range(2):
            back_tok(t, peer * 2 + q).wait()
        links.arrived(t * stride + 11)
    links.finish()
    yield


def step_kernel(
    outer, scale, count, mlp_count,
    act, wg_far, wu_far, wd_far, enc_far, enc_bias, dec_far, dec_bias, sizes,
    cen_out, code_out, back_out, grad_out, mse_out,
    wg, wu, wd, enc, dec, mlp, load_sems, *scratch,
):
    pairs = ((wg_far, wg), (wu_far, wu), (wd_far, wd), (enc_far, enc), (dec_far, dec))
    loads = [
        pltpu.make_async_copy(src, dst, load_sems.at[k]) for k, (src, dst) in enumerate(pairs)
    ]
    for load in loads:
        load.start()
    me, sg, tok = lax.axis_index("shard"), lax.axis_index("seg"), lax.axis_index("tok")
    core, group = sg % 2, sg // 2
    x, y, _ = square_of(me)
    greet(
        [{"shard": x}, {"shard": y}, {"seg": sg + 1 - 2 * core}, {"tok": 1 - tok}]
        + [{"seg": ((group + d) % outer) * 2 + core} for d in range(1, outer)]
    )
    loads[0].wait()
    loads[1].wait()
    first = mlp_steps(outer, loads[2].wait, act, wg, wu, wd, mlp, *scratch[:mlp_count])
    second = sae_steps(
        outer, scale, count, mlp, enc, enc_bias, dec, dec_bias, sizes,
        cen_out, code_out, back_out, grad_out, mse_out, *scratch[mlp_count:],
    )
    next(first)
    loads[3].wait()
    loads[4].wait()
    next(second)
    next(first)
    next(second)
    next(first)
    next(second)
    next(first)


def vmem(count):
    return [pl.BlockSpec(memory_space=pltpu.VMEM)] * count


def sems(*sizes):
    found = []
    for size in sizes:
        found += [pltpu.SemaphoreType.DMA((max(size, 1),))] * 2
    return found


def params(number):
    return pltpu.CompilerParams(
        collective_id=number, has_side_effects=True, vmem_limit_bytes=VMEM_BYTES
    )


def scatter_bufs(lead, rows, width):
    whole, half = lead + (rows, width), lead + (rows // 2, width)
    return [pltpu.VMEM(shape, BF16) for shape in (whole,) * 3 + (half,) * 2 + (whole,) * 2]


def step_call(act, wg, wu, wd, enc, enc_bias, dec, dec_bias, sizes):
    n, outer = lax.axis_size("shard"), lax.axis_size("seg") // 2
    tokens, far = act.shape[0], max(outer - 1, 1)
    rows, part = tokens // 2, tokens // 4
    chunk, width = wg.shape[1] // n, wd.shape[1]
    depth, latents, half = width * n, enc.shape[1], width * n // 2
    total = tokens * lax.axis_size("tok")
    shape = jax.ShapeDtypeStruct
    mlp_scratch = [
        *scatter_bufs((2,), rows, 2 * chunk),
        pltpu.VMEM((2, rows, chunk), F32),
        pltpu.VMEM((2, rows, chunk), F32),
        pltpu.VMEM((2, n, rows, chunk), BF16),
        pltpu.VMEM((2, rows, width), F32),
        pltpu.VMEM((2, part, width), F32),
        pltpu.VMEM((2, part, width), BF16),
        pltpu.VMEM((2, far, part, width), BF16),
        *sems(2 * (18 + outer)),
    ]
    sae_scratch = [
        pltpu.VMEM((tokens, depth), BF16),
        pltpu.VMEM((tokens, latents), F32),
        *scatter_bufs((2,), rows, width),
        pltpu.VMEM((tokens, width), F32),
        pltpu.VMEM((tokens, width), F32),
        pltpu.VMEM((2, far, part, width), BF16),
        pltpu.VMEM((far, tokens, width), BF16),
        pltpu.VMEM((tokens, depth), BF16),
        pltpu.VMEM((tokens, latents), F32),
        pltpu.VMEM((TILE, width), F32),
        pltpu.VMEM((n, 8, 128), F32),
        pltpu.VMEM((2, 8, 128), F32),
        *sems(30 + 4 * (outer - 1), 4),
    ]
    inside, outside = pl.BlockSpec(memory_space=pltpu.VMEM), pl.BlockSpec(memory_space=pl.ANY)
    return pl.pallas_call(
        functools.partial(
            step_kernel, outer, 1.0 / math.sqrt(total), total * depth, len(mlp_scratch)
        ),
        out_shape=(
            shape((2, tokens, half), BF16),
            shape((2, tokens, latents), BF16),
            shape((2, tokens, half), BF16),
            shape((2, tokens, latents), BF16),
            shape((8, 128), F32),
        ),
        in_specs=[
            inside, outside, outside, outside, outside, inside, outside, inside,
            pl.BlockSpec(memory_space=pltpu.SMEM),
        ],
        out_specs=tuple(vmem(5)),
        scratch_shapes=[
            *(pltpu.VMEM(value.shape, BF16) for value in (wg, wu, wd, enc, dec)),
            pltpu.VMEM((tokens, depth), BF16),
            pltpu.SemaphoreType.DMA((5,)),
            *mlp_scratch,
            *sae_scratch,
        ],
        compiler_params=params(0),
        name="step",
    )(act, wg, wu, wd, enc, enc_bias, dec, dec_bias, sizes)


def fits(activations, gate_weight, encoder_weight):
    n, segs, toks = lax.axis_size("shard"), lax.axis_size("seg"), lax.axis_size("tok")
    rows, width = activations.shape
    lanes = (width, gate_weight.shape[1] // n, encoder_weight.shape[1])
    return (
        toks == 2
        and n == 4
        and segs % 2 == 0
        and rows % (4 * TILE) == 0
        and all(size % 128 == 0 for size in lanes)
    )


def local(
    activations,
    gate_weight,
    up_weight,
    down_weight,
    encoder_weight,
    encoder_bias,
    decoder_weight,
    decoder_bias,
    segment_sizes,
):
    if not fits(activations, gate_weight, encoder_weight):
        return plain(
            activations,
            gate_weight,
            up_weight,
            down_weight,
            encoder_weight,
            encoder_bias,
            decoder_weight,
            decoder_bias,
            segment_sizes,
        )
    cen, codes, back, code_grad, mse = step_call(
        activations,
        gate_weight,
        up_weight,
        down_weight,
        encoder_weight,
        encoder_bias[None, :],
        decoder_weight,
        decoder_bias[None, :],
        segment_sizes,
    )

    def over_tokens(a, b):
        a, b = (value.reshape(-1, value.shape[2]) for value in (a, b))
        return lax.dot_general(a, b, (((0,), (0,)), ((), ())), preferred_element_type=F32)

    return over_tokens(cen, code_grad), over_tokens(codes, back), mse[0, :1]


def solution(mesh):
    in_specs = (
        P("tok", "shard"),
        P("shard", "seg"),
        P("shard", "seg"),
        P("seg", "shard"),
        P(None, ("seg", "shard")),
        P(("seg", "shard")),
        P(("seg", "shard"), None),
        P(),
        P(),
    )
    out_specs = (P("tok", ("seg", "shard")), P(("seg", "shard"), "tok"), P("seg"))
    return jax.shard_map(local, mesh=mesh, in_specs=in_specs, out_specs=out_specs, check_vma=False)
```

```python
import functools
import math

import jax
import jax.numpy as jnp
from jax import lax
from jax.experimental import pallas as pl
from jax.experimental.pallas import tpu as pltpu
from jax.sharding import PartitionSpec as P

MESH = pl.DeviceIdType.MESH
F32 = jnp.float32
BF16 = jnp.bfloat16
TILE = 32
VMEM_BYTES = 52 * 1024 * 1024


def carried_in(value, axis, join, neutral, backward):
    count, mine = (lax.axis_size(axis), lax.axis_index(axis))
    pieces = lax.all_gather(value, axis)
    if backward:
        pieces = pieces[::-1]
        mine = count - 1 - mine
    subtotal = jnp.full_like(value, 0) + jnp.asarray(neutral, value.dtype)

    def hop(position, subtotal):
        longer = join(subtotal, pieces[position])
        return jnp.where(position < mine, longer, subtotal)

    return lax.fori_loop(0, count - 1, hop, subtotal)


def plain(
    activations,
    gate_weight,
    up_weight,
    down_weight,
    encoder_weight,
    encoder_bias,
    decoder_weight,
    decoder_bias,
    segment_sizes,
):
    shard_index = lax.axis_index("shard")
    segment_index = lax.axis_index("seg")
    group_index = lax.axis_index("tok")
    tok_rows = activations.shape[0]
    width_slice = activations.shape[1]
    gate_part = jnp.dot(activations, gate_weight, preferred_element_type=jnp.float32)
    up_part = jnp.dot(activations, up_weight, preferred_element_type=jnp.float32)
    gate_total, up_total = lax.psum((gate_part, up_part), "shard")
    hidden = (jax.nn.gelu(gate_total, approximate=True) * up_total).astype(jnp.bfloat16)
    down_part = jnp.dot(hidden, down_weight, preferred_element_type=jnp.float32)
    mlp_slice = lax.psum(down_part, "seg").astype(jnp.bfloat16)
    mlp_full = lax.all_gather(mlp_slice, "shard", axis=1, tiled=True)
    width = mlp_full.shape[1]
    groups = lax.axis_size("tok")
    tokens_all = tok_rows * groups
    half_width = width // groups
    mlp_float = mlp_full.astype(jnp.float32)
    centered = (mlp_float - decoder_bias).astype(jnp.bfloat16)
    lat_count = encoder_weight.shape[1]
    segment_total = segment_sizes.shape[0]
    size_here = jnp.sum(jnp.where(jnp.arange(segment_total) == segment_index, segment_sizes, 0))
    latent_index = shard_index * lat_count + jnp.arange(lat_count)
    live_mask = latent_index < size_here
    pre_act = jnp.dot(centered, encoder_weight, preferred_element_type=jnp.float32) + encoder_bias
    latent_codes = jnp.where(live_mask, jax.nn.softplus(10.0 * pre_act) / 10.0, 0.0).astype(
        jnp.bfloat16
    )
    slope = jnp.where(live_mask, jax.nn.sigmoid(10.0 * pre_act), 0.0)
    codes_all = lax.all_gather(latent_codes, "tok", axis=0, tiled=True)
    centered_all = lax.all_to_all(centered, "tok", split_axis=1, concat_axis=0, tiled=True)
    columns = decoder_weight
    my_part = lax.psum_scatter(
        lax.dot_general(
            columns, latent_codes, (((0,), (1,)), ((), ())), preferred_element_type=jnp.float32
        ),
        "shard",
        scatter_dimension=0,
        tiled=True,
    )
    column_start = shard_index * width_slice
    target = lax.dynamic_slice_in_dim(mlp_float, column_start, width_slice, 1).T
    bias_slice = lax.dynamic_slice_in_dim(decoder_bias, column_start, width_slice, 0)[:, None]
    blank = jnp.zeros_like(my_part)
    earlier = carried_in(my_part, "seg", jnp.add, blank, False)
    errors = bias_slice + (earlier + my_part) - target
    total_square = lax.psum(jnp.sum(errors * errors), ("shard", "tok"))
    prefix_mse = (total_square / (tokens_all * width)).reshape(1)
    later = carried_in(errors, "seg", jnp.add, blank, True)
    back = ((later + errors) * (1.0 / math.sqrt(tokens_all))).astype(jnp.bfloat16)
    back_all = lax.all_gather(back, "tok", axis=1, tiled=True)
    piece = lax.all_gather(back_all, "shard", axis=0, tiled=True)
    columns = decoder_weight
    own_piece = lax.dynamic_slice_in_dim(piece, group_index * tok_rows, tok_rows, 1)
    code_acc = lax.dot_general(
        own_piece, columns, (((0,), (1,)), ((), ())), preferred_element_type=jnp.float32
    )
    grad_piece = lax.dot_general(
        codes_all, piece, (((0,), (1,)), ((), ())), preferred_element_type=jnp.float32
    )
    code_grad = (code_acc * slope).astype(jnp.bfloat16)
    code_grad_all = lax.all_gather(code_grad, "tok", axis=0, tiled=True)
    grad_encoder = lax.dot_general(
        centered_all, code_grad_all, (((0,), (0,)), ((), ())), preferred_element_type=jnp.float32
    )
    grad_decoder = lax.dynamic_slice_in_dim(grad_piece, group_index * half_width, half_width, 1)
    return (grad_encoder, grad_decoder, prefix_mse)


def send(src, dst, send_sem, recv_sem, **place):
    return pltpu.make_async_remote_copy(
        src_ref=src,
        dst_ref=dst,
        send_sem=send_sem,
        recv_sem=recv_sem,
        device_id=place,
        device_id_type=MESH,
    )


def greet(peers):
    barrier = pltpu.get_barrier_semaphore()
    for place in peers:
        pl.semaphore_signal(barrier, inc=1, device_id=place, device_id_type=MESH)
    pl.semaphore_wait(barrier, len(peers))


def by_rows(total, body):
    def step(i, carry):
        body(i * TILE)
        return carry

    lax.fori_loop(0, total // TILE, step, 0)


def tile_at(first):
    return pl.ds(pl.multiple_of(first, TILE), TILE)


def span(index, size):
    return pl.ds(pl.multiple_of(index * size, 128 if size % 128 == 0 else 32), size)


def dot(a, b):
    return jnp.dot(a, b, preferred_element_type=F32)


def dot_t(a, b):
    return lax.dot_general(a, b, (((1,), (1,)), ((), ())), preferred_element_type=F32)


def gelu_tanh(x):
    return x * (0.5 * (1.0 + jnp.tanh(math.sqrt(2.0 / math.pi) * (x + 0.044715 * (x * x * x)))))


class Links:
    def __init__(self, send_sems, recv_sems):
        self.sems, self.copies = (send_sems, recv_sems), {}

    def start(self, number, src, dst, **place):
        sent, got = (group.at[number] for group in self.sems)
        self.copies[number] = send(src, dst, sent, got, **place)
        self.copies[number].start()

    def arrived(self, *numbers):
        for number in numbers:
            self.copies[number].wait_recv()

    def finish(self):
        for copy in self.copies.values():
            copy.wait_send()


def square_of(me):
    x = me + 1 - 2 * (me % 2)
    y = (me + 2) % 4
    return x, y, (x + 2) % 4


def scatter_start(links, base, fill, square, half, bufs):
    x, y, corner = square
    to_corner, to_x, to_y, via_x, via_y, from_x, from_y = bufs
    top, low = pl.ds(0, half), pl.ds(half, half)
    fill(to_corner, corner)
    links.start(base, to_corner.at[top, :], via_x, shard=x)
    links.start(base + 1, to_corner.at[low, :], via_y, shard=y)
    fill(to_x, x)
    links.start(base + 2, to_x.at[top, :], from_x.at[top, :], shard=x)
    fill(to_y, y)
    links.start(base + 3, to_y.at[low, :], from_y.at[low, :], shard=y)


def scatter_forward(links, base, square, half, bufs):
    x, y, _ = square
    _, to_x, to_y, via_x, via_y, from_x, from_y = bufs
    top, low = pl.ds(0, half), pl.ds(half, half)

    def add_top(first):
        r = tile_at(first)
        to_y[r, :] = (to_y[r, :].astype(F32) + via_x[r, :].astype(F32)).astype(BF16)

    def add_low(first):
        r, q = tile_at(first), tile_at(half + first)
        to_x[q, :] = (to_x[q, :].astype(F32) + via_y[r, :].astype(F32)).astype(BF16)

    links.arrived(base)
    by_rows(half, add_top)
    links.start(base + 4, to_y.at[top, :], from_y.at[top, :], shard=y)
    links.arrived(base + 1)
    by_rows(half, add_low)
    links.start(base + 5, to_x.at[low, :], from_x.at[low, :], shard=x)


def scatter_wait(links, base):
    links.arrived(base + 2, base + 3, base + 4, base + 5)


def gather_start(links, base, block, me, square):
    x, y, _ = square
    links.start(base, block(me), block(me), shard=x)
    links.start(base + 1, block(me), block(me), shard=y)


def gather_pass_x(links, base, block, square):
    x, y, _ = square
    links.arrived(base)
    links.start(base + 2, block(x, 0), block(x, 0), shard=y)


def gather_pass_y(links, base, block, square):
    x, y, _ = square
    links.arrived(base + 1)
    links.start(base + 3, block(y, 1), block(y, 1), shard=x)


def mlp_steps(
    outer, down_ready, act, wg, wu, wd, out,
    to_corner, to_x, to_y, via_x, via_y, from_x, from_y,
    gate, up, hid, down, got, half, far, sent, arrived,
):
    me, sg = lax.axis_index("shard"), lax.axis_index("seg")
    core, group = sg % 2, sg // 2
    twin = sg + 1 - 2 * core
    square = square_of(me)
    x, y, corner = square
    chunk = wg.shape[1] // 4
    width = wd.shape[1]
    rows = act.shape[0] // 2
    part = rows // 2
    small = part // 2
    links = Links(sent, arrived)
    stride = 19 + outer - 1
    def bufs(t):
        return [b.at[t] for b in (to_corner, to_x, to_y, via_x, via_y, from_x, from_y)]

    def tokens(t):
        return act[t * rows : (t + 1) * rows, :]

    def partial_start(t):
        def fill(ref, p):
            ref[:, :chunk] = dot(tokens(t), wg[:, span(p, chunk)]).astype(BF16)
            ref[:, chunk:] = dot(tokens(t), wu[:, span(p, chunk)]).astype(BF16)

        scatter_start(links, t * stride, fill, square, part, bufs(t))

    def partial_forward(t):
        scatter_forward(links, t * stride, square, part, bufs(t))

    def partial_own(t):
        gate[t] = dot(tokens(t), wg[:, span(me, chunk)])
        up[t] = dot(tokens(t), wu[:, span(me, chunk)])

    def hid_block(t):
        def block(s, k=None):
            r = pl.ds(0, rows) if k is None else pl.ds(k * part, part)
            return hid.at[t, s, r, :]

        return block

    def hidden_start(t):
        scatter_wait(links, t * stride)

        def hidden_rows(first):
            r = tile_at(first)
            g = gate[t, r, :] + from_x[t, r, :chunk].astype(F32) + from_y[t, r, :chunk].astype(F32)
            u = up[t, r, :] + from_x[t, r, chunk:].astype(F32) + from_y[t, r, chunk:].astype(F32)
            hid[t, me, r, :] = (gelu_tanh(g) * u).astype(BF16)

        by_rows(rows, hidden_rows)
        gather_start(links, t * stride + 6, hid_block(t), me, square)

    def hidden_forward(t):
        gather_pass_x(links, t * stride + 6, hid_block(t), square)
        gather_pass_y(links, t * stride + 6, hid_block(t), square)

    def term(t, s):
        return dot(hid[t, s], wd[span(s, chunk), :])

    def down_near(t):
        down[t] = term(t, me) + term(t, x) + term(t, y)

    def down_start(t):
        links.arrived(t * stride + 8, t * stride + 9)
        down[t] += term(t, corner)
        links.start(t * stride + 10, down.at[t, span(1 - core, part), :], got.at[t], seg=twin)

    def far_start(t):
        links.arrived(t * stride + 10)

        def half_rows(first):
            r = tile_at(first)
            half[t, r, :] = (down[t, tile_at(core * part + first), :] + got[t, r, :]).astype(BF16)

        by_rows(part, half_rows)
        for d in range(1, outer):
            to = ((group + d) % outer) * 2 + core
            links.start(t * stride + 18 + d, half.at[t], far.at[t, d - 1], seg=to)

    def out_block(t):
        def block(s, k=None):
            first = t * rows + core * part
            if k is None:
                r = pl.ds(pl.multiple_of(first, 32), part)
            else:
                r = pl.ds(pl.multiple_of(first + k * small, 16), small)
            return out.at[r, span(s, width)]

        return block

    def twin_start(t, number, s):
        piece = out_block(t)(s)
        links.start(t * stride + 15 + number, piece, piece, seg=twin)

    def out_start(t):
        for d in range(1, outer):
            links.arrived(t * stride + 18 + d)

        def out_rows(first):
            r = tile_at(first)
            total = half[t, r, :].astype(F32)
            for d in range(outer - 1):
                total = total + far[t, d, r, :].astype(F32)
            out[tile_at(t * rows + core * part + first), span(me, width)] = total.astype(BF16)

        by_rows(part, out_rows)
        gather_start(links, t * stride + 11, out_block(t), me, square)
        twin_start(t, 0, me)

    def out_forward(t):
        gather_pass_x(links, t * stride + 11, out_block(t), square)
        twin_start(t, 1, x)
        gather_pass_y(links, t * stride + 11, out_block(t), square)
        twin_start(t, 2, y)

    def out_last(t):
        links.arrived(t * stride + 13, t * stride + 14)
        twin_start(t, 3, corner)

    partial_start(0)
    partial_forward(0)
    partial_start(1)
    partial_own(0)
    hidden_start(0)
    partial_forward(1)
    partial_own(1)
    hidden_forward(0)
    down_ready()
    down_near(0)
    hidden_start(1)
    down_start(0)
    far_start(0)
    hidden_forward(1)
    down_near(1)
    out_start(0)
    down_start(1)
    far_start(1)
    out_forward(0)
    out_last(0)
    out_start(1)
    links.arrived(*(15 + k for k in range(4)))
    yield
    out_forward(1)
    yield
    out_last(1)
    links.arrived(*(stride + 15 + k for k in range(4)))
    yield
    links.finish()
    yield


def sae_steps(
    outer, scale, count, mlp, enc, enc_bias, dec, dec_bias, sizes,
    cen_out, code_out, back_out, grad_out, mse_out,
    cen, slope, to_corner, to_x, to_y, via_x, via_y, from_x, from_y, mine, other, payload, far,
    back, acc, squares, square_in, square_tok, sent, arrived, back_sent, back_arrived,
):
    me, sg, tok = lax.axis_index("shard"), lax.axis_index("seg"), lax.axis_index("tok")
    core, group = sg % 2, sg // 2
    twin = sg + 1 - 2 * core
    peer = 1 - tok
    square = square_of(me)
    x, y, corner = square
    links = Links(sent, arrived)
    segments = outer * 2
    tokens, depth = mlp.shape
    width = depth // 4
    half_width = depth // 2
    rows = tokens // 2
    part = rows // 2
    stride = 12 + 2 * (outer - 1)
    near_square, far_square, tok_square = (2 * stride + k for k in range(3))
    code_link, cen_link, cen_twin = (2 * stride + 3 + 2 * k for k in range(3))
    def center_rows(first):
        r = tile_at(first)
        cen[r, :] = (mlp[r, :].astype(F32) - dec_bias[...]).astype(BF16)
        cen_out[0, r, :] = cen[r, span(tok, half_width)]

    def bufs(t):
        return [b.at[t] for b in (to_corner, to_x, to_y, via_x, via_y, from_x, from_y)]

    def half_of(t):
        return pl.ds(t * rows, rows)

    latents = enc.shape[1]
    step = 256 if latents % 256 == 0 else 128

    def encode(t):
        def columns(i, carry):
            c = span(i, step)
            pre = 10.0 * (dot(cen[half_of(t), :], enc[:, c]) + enc_bias[:, c])
            index = me * latents + i * step + lax.broadcasted_iota(jnp.int32, (1, step), 1)
            on = index < sizes[sg]
            soft = jnp.maximum(pre, 0.0) + jnp.log1p(jnp.exp(-jnp.abs(pre)))
            code_out[0, half_of(t), c] = jnp.where(on, soft / 10.0, 0.0).astype(BF16)
            slope[half_of(t), c] = jnp.where(on, jax.nn.sigmoid(pre), 0.0)
            return carry

        lax.fori_loop(0, latents // step, columns, 0)

    def part_start(t):
        def fill(ref, p):
            ref[...] = dot(code_out[0, half_of(t), :], dec[:, span(p, width)]).astype(BF16)

        scatter_start(links, t * stride, fill, square, part, bufs(t))

    def part_forward(t):
        scatter_forward(links, t * stride, square, part, bufs(t))

    def part_own(t):
        mine[half_of(t), :] = dot(code_out[0, half_of(t), :], dec[:, span(me, width)])

    def part_sum(t):
        scatter_wait(links, t * stride)

        def mine_rows(first):
            r, q = tile_at(first), tile_at(t * rows + first)
            mine[q, :] = mine[q, :] + from_x[t, r, :].astype(F32) + from_y[t, r, :].astype(F32)

        by_rows(rows, mine_rows)
        links.start(
            t * stride + 10, mine.at[half_of(t), :], other.at[half_of(t), :], seg=twin
        )

    def core_rows(t):
        return pl.ds(pl.multiple_of(t * rows + core * part, TILE), part)

    def far_start(t):
        links.arrived(t * stride + 10)
        for d in range(1, outer):
            to = (group + d) % outer
            later = to > group
            weight_mine = jnp.where(later, 1, segments - sg).astype(F32)
            weight_other = jnp.where(later, 1, segments - twin).astype(F32)

            def payload_rows(first, d=d, weight_mine=weight_mine, weight_other=weight_other):
                q = tile_at(t * rows + core * part + first)
                payload[t, d - 1, tile_at(first), :] = (
                    weight_mine * mine[q, :] + weight_other * other[q, :]
                ).astype(BF16)

            by_rows(part, payload_rows)
            links.start(
                t * stride + 11 + d,
                payload.at[t, d - 1],
                far.at[d - 1, core_rows(t), :],
                seg=to * 2 + core,
            )

    def far_pass(t):
        for d in range(1, outer):
            links.arrived(t * stride + 11 + d)
            piece = far.at[d - 1, core_rows(t), :]
            links.start(t * stride + 10 + outer + d, piece, piece, seg=twin)

    def cen_start(t):
        links.start(
            cen_link + t,
            cen.at[core_rows(t), span(peer, half_width)],
            cen_out.at[1, core_rows(t), :],
            tok=peer,
        )

    def cen_pass(t):
        links.arrived(cen_link + t)
        piece = cen_out.at[1, core_rows(t), :]
        links.start(cen_twin + t, piece, piece, seg=twin)

    def code_start(t):
        links.start(
            code_link + t,
            code_out.at[0, half_of(t), :],
            code_out.at[1, half_of(t), :],
            tok=peer,
        )

    ahead = (segments - sg).astype(F32)
    other_error = core.astype(F32)
    other_back = (segments - sg - 1 + core).astype(F32)
    bias_here = dec_bias[:, span(me, width)]

    def back_block(t):
        def block(s, k=None):
            r = half_of(t) if k is None else pl.ds(t * rows + k * part, part)
            return back.at[r, span(s, width)]

        return block

    def back_tok(t, s):
        q = s % 2
        return send(
            back_block(t)(s),
            back_out.at[1, half_of(t), span(q, width)],
            back_sent.at[t * 2 + q],
            back_arrived.at[t * 2 + q],
            tok=peer,
        )

    def pass_on(t, s):
        @pl.when(s // 2 == peer)
        def _():
            back_tok(t, s).start()

    def back_start(t):
        for d in range(1, outer):
            links.arrived(t * stride + 10 + outer + d)

        def error_rows(first):
            r = tile_at(t * rows + first)
            here, there = mine[r, :], other[r, :]
            base = bias_here - mlp[r, span(me, width)].astype(F32)
            after = jnp.zeros_like(here)
            for d in range(1, outer):
                before = ((group + outer - d) % outer < group).astype(F32)
                came = far[d - 1, r, :].astype(F32)
                base = base + before * came
                after = after + (1.0 - before) * came
            error = base + other_error * there + here
            squares[...] += error * error
            total = ahead * (base + here) + other_back * there + after
            back[r, span(me, width)] = (total * scale).astype(BF16)

        by_rows(rows, error_rows)
        gather_start(links, t * stride + 6, back_block(t), me, square)
        pass_on(t, me)

    def back_term(t, s):
        return dot_t(back[half_of(t), span(s, width)], dec[:, span(s, width)])

    def back_forward(t):
        gather_pass_x(links, t * stride + 6, back_block(t), square)
        pass_on(t, x)
        gather_pass_y(links, t * stride + 6, back_block(t), square)
        pass_on(t, y)

    def back_near(t):
        acc[half_of(t), :] = back_term(t, me) + back_term(t, x) + back_term(t, y)

    def back_last(t):
        links.arrived(t * stride + 8, t * stride + 9)
        pass_on(t, corner)
        acc[half_of(t), :] += back_term(t, corner)

        def grad_rows(first):
            r = tile_at(t * rows + first)
            grad_out[0, r, :] = (acc[r, :] * slope[r, :]).astype(BF16)

        by_rows(rows, grad_rows)
        links.start(
            t * stride + 11,
            grad_out.at[0, half_of(t), :],
            grad_out.at[1, half_of(t), :],
            tok=peer,
        )

    squares[...] = jnp.zeros_like(squares)
    by_rows(rows, center_rows)
    cen_start(0)
    encode(0)
    code_start(0)
    yield
    part_start(0)
    yield
    by_rows(rows, lambda first: center_rows(rows + first))
    cen_start(1)
    encode(1)
    part_forward(0)
    part_start(1)
    part_own(0)
    part_sum(0)
    part_forward(1)
    far_start(0)
    part_own(1)
    code_start(1)
    far_pass(0)
    part_sum(1)
    back_start(0)
    far_start(1)
    back_forward(0)
    far_pass(1)
    back_near(0)
    back_start(1)
    back_last(0)
    square_sum = jnp.sum(squares[...]) / count
    square_in[0] = jnp.full(square_in.shape[1:], square_sum, F32)
    links.start(near_square, square_in.at[0], square_in.at[1], shard=x)
    back_forward(1)
    back_near(1)
    links.arrived(near_square)
    square_in[2] = square_in[0] + square_in[1]
    links.start(far_square, square_in.at[2], square_in.at[3], shard=y)
    back_last(1)
    links.arrived(far_square)
    square_tok[0] = square_in[2] + square_in[3]
    links.start(tok_square, square_tok.at[0], square_tok.at[1], tok=peer)
    for t in range(2):
        cen_pass(t)

    def own_back(first):
        r = tile_at(first)
        back_out[0, r, :] = back[r, span(tok, half_width)]

    by_rows(tokens, own_back)
    links.arrived(tok_square)
    mse_out[...] = square_tok[0] + square_tok[1]
    for t in range(2):
        links.arrived(code_link + t, cen_twin + t)
        for q in range(2):
            back_tok(t, peer * 2 + q).wait()
        links.arrived(t * stride + 11)
    links.finish()
    yield


def step_kernel(
    outer, scale, count, mlp_count,
    act, wg_far, wu_far, wd_far, enc_far, enc_bias, dec_far, dec_bias, sizes,
    cen_out, code_out, back_out, grad_out, mse_out,
    wg, wu, wd, enc, dec, mlp, load_sems, *scratch,
):
    pairs = ((wg_far, wg), (wu_far, wu), (wd_far, wd), (enc_far, enc), (dec_far, dec))
    loads = [
        pltpu.make_async_copy(src, dst, load_sems.at[k]) for k, (src, dst) in enumerate(pairs)
    ]
    for load in loads:
        load.start()
    me, sg, tok = lax.axis_index("shard"), lax.axis_index("seg"), lax.axis_index("tok")
    core, group = sg % 2, sg // 2
    x, y, _ = square_of(me)
    greet(
        [{"shard": x}, {"shard": y}, {"seg": sg + 1 - 2 * core}, {"tok": 1 - tok}]
        + [{"seg": ((group + d) % outer) * 2 + core} for d in range(1, outer)]
    )
    loads[0].wait()
    loads[1].wait()
    first = mlp_steps(outer, loads[2].wait, act, wg, wu, wd, mlp, *scratch[:mlp_count])
    second = sae_steps(
        outer, scale, count, mlp, enc, enc_bias, dec, dec_bias, sizes,
        cen_out, code_out, back_out, grad_out, mse_out, *scratch[mlp_count:],
    )
    next(first)
    loads[3].wait()
    loads[4].wait()
    next(second)
    next(first)
    next(second)
    next(first)
    next(second)
    next(first)


def vmem(count):
    return [pl.BlockSpec(memory_space=pltpu.VMEM)] * count


def sems(*sizes):
    found = []
    for size in sizes:
        found += [pltpu.SemaphoreType.DMA((max(size, 1),))] * 2
    return found


def params(number):
    return pltpu.CompilerParams(
        collective_id=number, has_side_effects=True, vmem_limit_bytes=VMEM_BYTES
    )


def scatter_bufs(lead, rows, width):
    whole, half = lead + (rows, width), lead + (rows // 2, width)
    return [pltpu.VMEM(shape, BF16) for shape in (whole,) * 3 + (half,) * 2 + (whole,) * 2]


def step_call(act, wg, wu, wd, enc, enc_bias, dec, dec_bias, sizes):
    n, outer = lax.axis_size("shard"), lax.axis_size("seg") // 2
    tokens, far = act.shape[0], max(outer - 1, 1)
    rows, part = tokens // 2, tokens // 4
    chunk, width = wg.shape[1] // n, wd.shape[1]
    depth, latents, half = width * n, enc.shape[1], width * n // 2
    total = tokens * lax.axis_size("tok")
    shape = jax.ShapeDtypeStruct
    mlp_scratch = [
        *scatter_bufs((2,), rows, 2 * chunk),
        pltpu.VMEM((2, rows, chunk), F32),
        pltpu.VMEM((2, rows, chunk), F32),
        pltpu.VMEM((2, n, rows, chunk), BF16),
        pltpu.VMEM((2, rows, width), F32),
        pltpu.VMEM((2, part, width), F32),
        pltpu.VMEM((2, part, width), BF16),
        pltpu.VMEM((2, far, part, width), BF16),
        *sems(2 * (18 + outer)),
    ]
    sae_scratch = [
        pltpu.VMEM((tokens, depth), BF16),
        pltpu.VMEM((tokens, latents), F32),
        *scatter_bufs((2,), rows, width),
        pltpu.VMEM((tokens, width), F32),
        pltpu.VMEM((tokens, width), F32),
        pltpu.VMEM((2, far, part, width), BF16),
        pltpu.VMEM((far, tokens, width), BF16),
        pltpu.VMEM((tokens, depth), BF16),
        pltpu.VMEM((tokens, latents), F32),
        pltpu.VMEM((TILE, width), F32),
        pltpu.VMEM((n, 8, 128), F32),
        pltpu.VMEM((2, 8, 128), F32),
        *sems(33 + 4 * (outer - 1), 4),
    ]
    inside, outside = pl.BlockSpec(memory_space=pltpu.VMEM), pl.BlockSpec(memory_space=pl.ANY)
    return pl.pallas_call(
        functools.partial(
            step_kernel, outer, 1.0 / math.sqrt(total), total * depth, len(mlp_scratch)
        ),
        out_shape=(
            shape((2, tokens, half), BF16),
            shape((2, tokens, latents), BF16),
            shape((2, tokens, half), BF16),
            shape((2, tokens, latents), BF16),
            shape((8, 128), F32),
        ),
        in_specs=[
            inside, outside, outside, outside, outside, inside, outside, inside,
            pl.BlockSpec(memory_space=pltpu.SMEM),
        ],
        out_specs=tuple(vmem(5)),
        scratch_shapes=[
            *(pltpu.VMEM(value.shape, BF16) for value in (wg, wu, wd, enc, dec)),
            pltpu.VMEM((tokens, depth), BF16),
            pltpu.SemaphoreType.DMA((5,)),
            *mlp_scratch,
            *sae_scratch,
        ],
        compiler_params=params(0),
        name="step",
    )(act, wg, wu, wd, enc, enc_bias, dec, dec_bias, sizes)


def fits(activations, gate_weight, encoder_weight):
    n, segs, toks = lax.axis_size("shard"), lax.axis_size("seg"), lax.axis_size("tok")
    rows, width = activations.shape
    lanes = (width, gate_weight.shape[1] // n, encoder_weight.shape[1])
    return (
        toks == 2
        and n == 4
        and segs % 2 == 0
        and rows % (4 * TILE) == 0
        and all(size % 128 == 0 for size in lanes)
    )


def local(
    activations,
    gate_weight,
    up_weight,
    down_weight,
    encoder_weight,
    encoder_bias,
    decoder_weight,
    decoder_bias,
    segment_sizes,
):
    if not fits(activations, gate_weight, encoder_weight):
        return plain(
            activations,
            gate_weight,
            up_weight,
            down_weight,
            encoder_weight,
            encoder_bias,
            decoder_weight,
            decoder_bias,
            segment_sizes,
        )
    cen, codes, back, code_grad, mse = step_call(
        activations,
        gate_weight,
        up_weight,
        down_weight,
        encoder_weight,
        encoder_bias[None, :],
        decoder_weight,
        decoder_bias[None, :],
        segment_sizes,
    )

    def over_tokens(a, b):
        a, b = (value.reshape(-1, value.shape[2]) for value in (a, b))
        return lax.dot_general(a, b, (((0,), (0,)), ((), ())), preferred_element_type=F32)

    return over_tokens(cen, code_grad), over_tokens(codes, back), mse[0, :1]


def solution(mesh):
    in_specs = (
        P("tok", "shard"),
        P("shard", "seg"),
        P("shard", "seg"),
        P("seg", "shard"),
        P(None, ("seg", "shard")),
        P(("seg", "shard")),
        P(("seg", "shard"), None),
        P(),
        P(),
    )
    out_specs = (P("tok", ("seg", "shard")), P(("seg", "shard"), "tok"), P("seg"))
    return jax.shard_map(local, mesh=mesh, in_specs=in_specs, out_specs=out_specs, check_vma=False)
```
